256 devices in a mesh: section: 8 (over x, core), dp: 32 (over z, y).
Axes of the slice: x: 4, y: 4, z: 8, core: 2. Of those that a mesh axis runs over, the one named last changes fastest.
Arguments:
- saved_inputs: bfloat16 [8, 4, 32, 40, 14848], P('section', None, 'dp'), may hold values from -40 to 40, as said below
- example_ids: int32 [4, 32, 40], P(None, 'dp'), may hold values from 0 to 1, never falling along the last dimension, each value on 1 to 30 neighbouring positions
- loss_grads: bfloat16 [4, 32, 40, 14848], P(None, 'dp', None, 'section'), may hold values from -0.041 to 0.041, as said below
- w_down: bfloat16 [8, 14848, 128], P('section', 'dp'), may hold values from -0.049072266 to 0.049072266
- w_up: bfloat16 [8, 14848, 128], P('section', 'dp'), may hold values from -0.5 to 0.5
- run_down: float32 [8, 14848, 128], P('section', 'dp'), may hold values from -6 to 6
- run_up: float32 [8, 14848, 128], P('section', 'dp'), may hold values from -6 to 6
- noise_down: float32 [8, 14848, 128], P('section', 'dp'), may hold values from -6 to 6
- noise_up: float32 [8, 14848, 128], P('section', 'dp'), may hold values from -6 to 6
Outputs:
- new_down: float32 [8, 14848, 128], P('section', 'dp')
- new_up: float32 [8, 14848, 128], P('section', 'dp')
- example_norms: float32 [4, 32, 2], P(None, 'dp')
The draws below stay inside these ranges and needn't reach their ends.
Inputs may be any that keep to these rules, and one draw needn't show every extreme that they name: `saved_inputs`: activations of order one with scales that differ from token to token and feature to feature. `loss_grads`: gradients of order one thousandth with scales that differ from token to token and feature to feature. `example_ids`: each of the 2 examples of a row and microbatch covers 40 - 1 * 30 to 30 positions.
All inputs are finite; a program needn't handle non-finite values.
Results may differ from the reference program's by a relative error of at most 0.025.
Values may be sent and summed in bfloat16 or wider, within the bound.
No kernel may reach another device: no remote copies, remote signals or barrier semaphores. Data moves between devices by JAX's collectives and lax.ppermute only.
A program may use at most 128 MiB of HBM per device.

```python
import math
import jax
import jax.numpy as jnp
import numpy as np
from jax import lax

D = 14848
R = 128
MICRO = 4
MB_TOK = 40
EX = 2
MOST = 30
SECTIONS = 8
ROWS = 32


def scaled_field(key, base, row_lo, row_hi):
    shape = base.shape
    key_rows, key_cols = jax.random.split(key, 2)
    row_scale = jnp.exp(jax.random.uniform(key_rows, shape[:-1] + (1,), jnp.float32, jnp.log(row_lo), jnp.log(row_hi)))
    col_scale = jnp.exp(jax.random.uniform(key_cols, (shape[-1],), jnp.float32, jnp.log(0.5), jnp.log(2.0)))
    return jnp.clip(base * row_scale * col_scale, -40.0, 40.0)


def draw_saved_inputs(key, part):
    key = jax.random.fold_in(key, 11)
    key_base, key_field = jax.random.split(key)
    shape = (SECTIONS, MICRO, ROWS, MB_TOK, D)
    base = jnp.clip(jax.random.normal(key_base, shape, jnp.float32), -5.0, 5.0)
    values = scaled_field(key_field, base, 0.5, 5.0)
    return values.astype(jnp.bfloat16)


def draw_loss_grads(key, part):
    key = jax.random.fold_in(key, 23)
    key_base, key_field = jax.random.split(key)
    shape = (MICRO, ROWS, MB_TOK, D)
    base = jnp.clip(jax.random.normal(key_base, shape, jnp.float32), -5.0, 5.0)
    values = scaled_field(key_field, base, 0.5, 5.0)
    return (values * 0.001).astype(jnp.bfloat16)


def block_scale(stream_key, shape, cuts, least, top_value):
    def one(dim, blocks):
        draws = jax.random.uniform(jax.random.fold_in(jax.random.fold_in(stream_key, 6), dim), (blocks,), jnp.float32, least / len(cuts), top_value / len(cuts))
        return jnp.repeat(jnp.exp(draws), shape[dim] // blocks).reshape((-1,) + (1,) * (len(shape) - dim - 1))

    loudness = one(*cuts[0])
    for cut in cuts[1:]:
        loudness = loudness * one(*cut)
    return loudness


def profile(number_of, total, bound, slope):
    portions = [(1 << 20) // math.isqrt(standing ** slope) + 1 for standing in range(2, number_of + 1)]
    surplus, given = total - bound - (number_of - 1), [1] * (number_of - 1)
    while surplus > 0:
        free = [i for i in range(number_of - 1) if given[i] < bound]
        mass, left = sum([portions[i] for i in free]), surplus
        for i in free:
            more = min(bound - given[i], max(1, left * portions[i] // mass), surplus)
            given[i] = given[i] + more
            surplus = surplus - more
    return np.array([bound] + given)


def uneven_parts(stream_key, amount, total, most, lean):
    if amount == 2:
        one = jax.random.randint(stream_key, (), max(1, total - most), min(most, total - 1) + 1)
        return jnp.stack([one, total - one])
    lengths = jnp.asarray(profile(amount, total, most, lean), jnp.int32)
    pairs = (amount - 1) // 2
    donor, sink = lengths[1:1 + 2 * pairs:2], lengths[2:2 + 2 * pairs:2]
    slack = jnp.minimum(donor - 1, most - sink)
    moved = jax.random.randint(jax.random.fold_in(stream_key, 1), (pairs,), 0, 1 << 20) % (slack + 1)
    lengths = lengths.at[1:1 + 2 * pairs:2].set(donor - moved).at[2:2 + 2 * pairs:2].set(sink + moved)
    return lengths[jax.random.permutation(jax.random.fold_in(stream_key, 2), amount)]


def centred(key, shape, scale, limit, cuts=(), kind=jnp.bfloat16):
    level = block_scale(key, shape, cuts, -0.22, 0.18) if cuts else 1.0
    values = jax.random.normal(key, shape, jnp.float32) * scale * level
    return jnp.minimum(jnp.maximum(values, -limit), limit).astype(kind)


def setup_inputs(seed: int = 0) -> dict:
    seeds = jax.random.split(jax.random.key(seed), 10)
    return {
        "saved_inputs": draw_saved_inputs(jax.random.fold_in(seeds[9], 71), 0),
        "example_ids": jax.vmap(lambda own: jnp.searchsorted(jnp.cumsum(uneven_parts(own, EX, MB_TOK, MOST, 2)), jnp.arange(MB_TOK), side="right"))(jax.random.split(seeds[1], MICRO * ROWS)).reshape((MICRO, ROWS, MB_TOK)).astype(jnp.int32),
        "loss_grads": draw_loss_grads(jax.random.fold_in(seeds[9], 71), 0),
        "w_down": centred(seeds[3], (SECTIONS, D, R), (0.9 * D ** -0.5), 0.049072266, ((0, 8), (1, 32))),
        "w_up": centred(seeds[4], (SECTIONS, D, R), R ** -0.5, 0.5, ((0, 8), (1, 32))),
        "run_down": centred(seeds[5], (SECTIONS, D, R), 1.0, 6.0, ((0, 8), (1, 32)), jnp.float32),
        "run_up": centred(seeds[6], (SECTIONS, D, R), 1.0, 6.0, ((0, 8), (1, 32)), jnp.float32),
        "noise_down": centred(seeds[7], (SECTIONS, D, R), 1.0, 6.0, ((0, 8), (1, 32)), jnp.float32),
        "noise_up": centred(seeds[8], (SECTIONS, D, R), 1.0, 6.0, ((0, 8), (1, 32)), jnp.float32),
    }


clip_bound = 400.0

def gelu_parts(hidden):
    normal_cdf = 0.5 * (1.0 + jax.scipy.special.erf(hidden * 0.7071067811865476))
    normal_pdf = jnp.exp(-0.5 * hidden * hidden) * 0.3989422804014327
    return (hidden * normal_cdf, normal_cdf + hidden * normal_pdf)

def grouped_norms(block_in, hidden_grad, activated, grad_out, member):

    def gram_of(values):
        wide = values.astype(jnp.float32)
        return jnp.einsum('gtd,gsd->gts', wide, wide)
    products = gram_of(block_in) * gram_of(hidden_grad) + gram_of(activated) * gram_of(grad_out)
    return jnp.einsum('gte,gts,gse->ge', member, products, member)

def reference(saved_inputs, example_ids, loss_grads, w_down, w_up, run_down, run_up, noise_down, noise_up):
    groups = MICRO * ROWS
    member = (example_ids.reshape(groups, MB_TOK)[:, :, None] == jnp.arange(EX, dtype=jnp.int32)[None, None, :]).astype(jnp.float32)

    def section_step(grad_out, section_index):
        block_in = lax.dynamic_index_in_dim(saved_inputs, section_index, 0, keepdims=False).reshape(-1, D)
        down_mat = lax.dynamic_index_in_dim(w_down, section_index, 0, keepdims=False)
        up_mat = lax.dynamic_index_in_dim(w_up, section_index, 0, keepdims=False)
        flat_grad = grad_out.reshape(-1, D)
        hidden = jnp.dot(block_in, down_mat, preferred_element_type=jnp.float32)
        gated, gate_slope = gelu_parts(hidden)
        activated = gated.astype(jnp.bfloat16)
        branch_grad = jnp.dot(flat_grad, up_mat, preferred_element_type=jnp.float32)
        hidden_grad = (branch_grad * gate_slope).astype(jnp.bfloat16)
        passed = flat_grad.astype(jnp.float32) + lax.dot_general(hidden_grad, down_mat, (((1,), (1,)), ((), ())), preferred_element_type=jnp.float32)
        passed = passed.astype(jnp.bfloat16)
        norms_here = grouped_norms(block_in.reshape(groups, MB_TOK, D), hidden_grad.reshape(groups, MB_TOK, R), activated.reshape(groups, MB_TOK, R), flat_grad.reshape(groups, MB_TOK, D), member)
        return (passed.reshape(grad_out.shape), (grad_out, activated.reshape(MICRO, ROWS, MB_TOK, R), hidden_grad.reshape(MICRO, ROWS, MB_TOK, R), norms_here))
    order = jnp.arange(SECTIONS - 1, -1, -1, dtype=jnp.int32)
    _, (grads_all, acts_all, hiddens_all, norms_all) = lax.scan(section_step, loss_grads, order)
    grads_all = grads_all[::-1]
    acts_all = acts_all[::-1]
    hiddens_all = hiddens_all[::-1]
    summed = lax.optimization_barrier(jnp.sum(norms_all, axis=0)).reshape(MICRO, ROWS, EX)
    example_norms = jnp.sqrt(summed)
    clip_scale = jnp.minimum(1.0, clip_bound * lax.rsqrt(summed))
    member_full = member.reshape(MICRO, ROWS, MB_TOK, EX)
    token_scale = lax.optimization_barrier(jnp.sum(member_full * clip_scale[:, :, None, :], axis=-1))

    def section_grads(section_index):
        block_in = lax.dynamic_index_in_dim(saved_inputs, section_index, 0, keepdims=False)
        grad_out = lax.dynamic_index_in_dim(grads_all, section_index, 0, keepdims=False)
        hidden_grad = lax.dynamic_index_in_dim(hiddens_all, section_index, 0, keepdims=False)
        activated = lax.dynamic_index_in_dim(acts_all, section_index, 0, keepdims=False)
        scaled_hidden = (hidden_grad.astype(jnp.float32) * token_scale[..., None]).astype(jnp.bfloat16)
        scaled_act = (activated.astype(jnp.float32) * token_scale[..., None]).astype(jnp.bfloat16)

        def per_row(running, row_index):
            row_in = lax.dynamic_index_in_dim(block_in, row_index, 1, keepdims=False).reshape(-1, D)
            row_grad = lax.dynamic_index_in_dim(grad_out, row_index, 1, keepdims=False).reshape(-1, D)
            row_hidden = lax.dynamic_index_in_dim(scaled_hidden, row_index, 1, keepdims=False).reshape(-1, R)
            row_act = lax.dynamic_index_in_dim(scaled_act, row_index, 1, keepdims=False).reshape(-1, R)
            part_down = lax.dot_general(row_in, row_hidden, (((0,), (0,)), ((), ())), preferred_element_type=jnp.float32)
            part_up = lax.dot_general(row_grad, row_act, (((0,), (0,)), ((), ())), preferred_element_type=jnp.float32)
            part_down = lax.optimization_barrier(part_down.astype(jnp.bfloat16)).astype(jnp.float32)
            part_up = lax.optimization_barrier(part_up.astype(jnp.bfloat16)).astype(jnp.float32)
            return ((running[0] + part_down, running[1] + part_up), None)
        start = (jnp.zeros((D, R), jnp.float32), jnp.zeros((D, R), jnp.float32))
        totals, _ = lax.scan(per_row, start, jnp.arange(ROWS, dtype=jnp.int32))
        return totals
    grad_down, grad_up = lax.map(section_grads, jnp.arange(SECTIONS, dtype=jnp.int32))
    new_down = run_down + grad_down + noise_down
    new_up = run_up + grad_up + noise_up
    return (new_down, new_up, example_norms)
```

```python
import jax
import jax.numpy as jnp
from jax import lax
from jax.sharding import PartitionSpec as P

EX = 2
NZ, NY = 8, 4
NX, NC = 4, 2

clip_bound = 400.0
bf16 = jnp.bfloat16
f32 = jnp.float32


def shift_z(value, d):
    pairs = [(z * NY + y, (z + d) % NZ * NY + y) for z in range(NZ) for y in range(NY)]
    return lax.ppermute(value, "dp", pairs)


def shift_y(value, d):
    pairs = [(z * NY + y, z * NY + (y + d) % NY) for z in range(NZ) for y in range(NY)]
    return lax.ppermute(value, "dp", pairs)


def shift_x(value, d):
    pairs = [(x * NC + c, (x + d) % NX * NC + c) for x in range(NX) for c in range(NC)]
    return lax.ppermute(value, "section", pairs)


def swap_core(value):
    return lax.ppermute(value, "section", [(s, s ^ 1) for s in range(NX * NC)])


def pick(value, index, axis=0):
    return lax.dynamic_index_in_dim(value, index, axis, keepdims=False)


def put(buffer, value, index, axis=0):
    return lax.dynamic_update_index_in_dim(buffer, value, index, axis)


def section_gather(value, x, c):
    held = jnp.zeros((NX,) + value.shape, value.dtype)
    held = put(held, value, x)
    held = put(held, shift_x(value, 1), (x + NX - 1) % NX)
    held = put(held, shift_x(value, -1), (x + 1) % NX)
    held = put(held, shift_x(value, 2), (x + 2) % NX)
    other = swap_core(held)
    even = jnp.where(c == 0, held, other)
    odd = jnp.where(c == 0, other, held)
    return jnp.stack([even, odd], axis=1).reshape((NX * NC,) + value.shape)


def loss_gather(value, x, c):
    half = value.shape[0] // 2
    before = shift_x(value, 1)
    after = shift_x(value, -1)
    across = jnp.concatenate([shift_x(before[:half], 1), shift_x(after[half:], -1)], axis=0)
    full = jnp.zeros((NX * NC,) + value.shape, value.dtype)
    for piece, place in ((value, x), (before, x + NX - 1), (after, x + 1), (across, x + 2)):
        place = place % NX
        full = put(full, piece, place * NC + c)
        full = put(full, swap_core(piece), place * NC + 1 - c)
    return full


def gather_y_then_z(block, z, y):
    quad = jnp.zeros((NY,) + block.shape, block.dtype)
    quad = put(quad, block, y)
    quad = put(quad, shift_y(block, 1), (y + NY - 1) % NY)
    quad = put(quad, shift_y(block, -1), (y + 1) % NY)
    quad = put(quad, shift_y(block, 2), (y + 2) % NY)
    full = jnp.zeros((NZ,) + quad.shape, block.dtype)
    full = put(full, quad, z)
    up = down = quad
    for step in range(1, NZ // 2):
        up, down = (shift_z(up, 1), shift_z(down, -1))
        full = put(full, up, (z + NZ - step) % NZ)
        full = put(full, down, (z + step) % NZ)
    half = NY // 2
    up, down = (shift_z(up[:half], 1), shift_z(down[half:], -1))
    return put(full, jnp.concatenate([up, down], axis=0), (z + NZ // 2) % NZ)


def gather_z_then_y(block, z, y):
    octet = jnp.zeros((NZ,) + block.shape, block.dtype)
    octet = put(octet, block, z)
    up = down = block
    for step in range(1, NZ // 2):
        up, down = (shift_z(up, 1), shift_z(down, -1))
        octet = put(octet, up, (z + NZ - step) % NZ)
        octet = put(octet, down, (z + step) % NZ)
    cut = block.shape[0] // 32 * 16
    up, down = (shift_z(up[:cut], 1), shift_z(down[cut:], -1))
    octet = put(octet, jnp.concatenate([up, down], axis=0), (z + NZ // 2) % NZ)
    full = jnp.zeros((NZ, NY) + block.shape, block.dtype)
    full = put(full, octet, y, 1)
    before, after = (shift_y(octet, 1), shift_y(octet, -1))
    full = put(full, before, (y + NY - 1) % NY, 1)
    full = put(full, after, (y + 1) % NY, 1)
    half = NZ // 2
    across = jnp.concatenate([shift_y(before[:half], 1), shift_y(after[half:], -1)], axis=0)
    return put(full, across, (y + 2) % NY, 1)


def add(*values):
    total = values[0].astype(f32)
    for value in values[1:]:
        total = total + value.astype(f32)
    return total


def scatter_z(parts, z, cut):
    ends = ((0, cut), (cut, parts.shape[1]))
    flows = []
    for sign, (low, high) in zip((1, -1), ends):
        far = pick(parts, (z + NZ // 2) % NZ)
        flow = shift_z(far[low:high], sign)
        for dist in range(NZ // 2 - 1, 0, -1):
            own = pick(parts, (z + NZ + sign * dist) % NZ)
            if dist == NZ // 2 - 1:
                padding = [(low, parts.shape[1] - high)] + [(0, 0)] * (flow.ndim - 1)
                flow = jnp.pad(flow, padding)
            flow = shift_z(add(own, flow).astype(bf16), sign)
        flows.append(flow)
    return add(pick(parts, z), *flows)


def scatter_z_then_y(parts, z, y):
    mine = scatter_z(parts, z, NY // 2)
    sent = mine.astype(bf16)
    pieces = [shift_y(pick(sent, (y + d) % NY), d) for d in (1, -1 % NY, 2)]
    return add(pick(mine, y), *pieces)


def scatter_y_then_z(parts, z, y):
    half = NZ // 2
    far = pick(parts, (y + 2) % NY, 1)
    up = jnp.pad(shift_y(far[:half], 1), ((0, half), (0, 0), (0, 0)))
    down = jnp.pad(shift_y(far[half:], -1), ((half, 0), (0, 0), (0, 0)))
    up = shift_y(add(pick(parts, (y + 1) % NY, 1), up).astype(bf16), 1)
    down = shift_y(add(pick(parts, (y + NY - 1) % NY, 1), down).astype(bf16), -1)
    mine = add(pick(parts, y, 1), up, down).astype(bf16)
    return scatter_z(mine, z, mine.shape[1] // 32 * 16)


def sum_everywhere(parts):
    count = lax.axis_size("dp")
    rows, width = parts.shape
    split = parts.astype(bf16).reshape(count, rows // count, width)
    arrived = lax.all_to_all(split, "dp", 0, 0)
    summed = jnp.sum(arrived.astype(f32), axis=0).astype(bf16)
    sent = jnp.broadcast_to(summed[None], split.shape)
    return lax.all_to_all(sent, "dp", 0, 0).reshape(rows, width)


def gelu_parts(hidden):
    normal_cdf = 0.5 * (1.0 + jax.scipy.special.erf(hidden * 0.7071067811865476))
    normal_pdf = jnp.exp(-0.5 * hidden * hidden) * 0.3989422804014327
    return (hidden * normal_cdf, normal_cdf + hidden * normal_pdf)


def mm(subs, *operands):
    return jnp.einsum(subs, *operands, preferred_element_type=f32)


def shards(
    saved_inputs, example_ids, loss_grads, w_down, w_up, run_down, run_up, noise_down, noise_up
):
    sections = lax.axis_size("section")
    section = lax.axis_index("section")
    row = lax.axis_index("dp")
    x, c = (section // NC, section % NC)
    z, y = (row // NY, row % NY)
    order = jnp.arange(sections)
    inputs = saved_inputs[0, :, 0]
    micro_count, tok_count, model_width = inputs.shape
    tokens = micro_count * tok_count
    bottleneck = w_down.shape[2]
    flat_in = inputs.reshape(tokens, model_width)
    loss_own = loss_grads[:, 0]
    slice_width = loss_own.shape[2]
    own_down, own_up = (w_down[0], w_up[0])

    down_full = gather_y_then_z(own_down, z, y).reshape(model_width, bottleneck)
    up_full = gather_z_then_y(own_up, z, y).reshape(model_width, bottleneck)
    loss_full = loss_gather(loss_own.reshape(tokens, slice_width), x, c)
    down_rows = section_gather(own_down, x, c)

    later = (order > section)[:, None, None]
    cross = jnp.where(
        later, mm("skm,kn->smn", down_rows, own_up), mm("skm,kn->smn", down_rows, own_down)
    )
    cross = sum_everywhere(cross.reshape(sections * bottleneck, bottleneck))
    cross = section_gather(cross.reshape(sections, bottleneck, bottleneck), x, c)

    hidden = mm("td,dk->tk", flat_in, down_full)
    gated, slope = gelu_parts(hidden)
    up_slices = up_full.reshape(sections, slice_width, bottleneck)
    down_slices = down_full.reshape(sections, slice_width, bottleneck)
    loss_up = jnp.sum(mm("itd,idk->itk", loss_full, up_slices), axis=0)
    loss_down = jnp.sum(mm("itd,idk->itk", loss_full, down_slices), axis=0)

    shared = jnp.stack([gated.astype(bf16), slope.astype(bf16), loss_up.astype(bf16)])
    shared = section_gather(shared, x, c)
    acts, slopes, branch = (shared[:, 0], shared[:, 1], shared[:, 2].astype(f32))

    grads = [None] * sections
    for s in range(sections - 1, -1, -1):
        grads[s] = (branch[s] * slopes[s].astype(f32)).astype(bf16)
        if s:
            step = mm("tm,smn->stn", grads[s], cross[:s, s])
            branch = branch[:s] + step
    grads = jnp.stack(grads)
    own_grad, own_act = (pick(grads, section), pick(acts, section))

    weight = jnp.where(order > section, 1.0, jnp.where(order == section, 0.5, 0.0)).astype(bf16)
    mixed = mm("stn,smn->tm", grads * weight[:, None, None], pick(cross, section, 1))
    mixed = (loss_down + mixed).astype(bf16).reshape(micro_count, tok_count, bottleneck)
    grad_micro = own_grad.reshape(micro_count, tok_count, bottleneck)
    step_gram = mm("btk,buk->btu", mixed, grad_micro)
    step_gram = step_gram + jnp.swapaxes(step_gram, 1, 2)
    acts_micro = acts.reshape(sections, micro_count, tok_count, bottleneck)
    act_grams = mm("sbtk,sbuk->sbtu", acts_micro, acts_micro)
    before = (order < section).astype(f32)
    products = (
        mm("btd,bud->btu", inputs, inputs) * mm("btk,buk->btu", grad_micro, grad_micro)
        + mm("btd,bud->btu", loss_own, loss_own) * jnp.sum(act_grams, axis=0)
        + step_gram * jnp.sum(act_grams * before[:, None, None, None], axis=0)
    )
    example_rows = example_ids[:, 0]
    member = (example_rows[:, :, None] == jnp.arange(EX, dtype=jnp.int32)).astype(f32)
    across_u = jnp.sum(products[..., None] * member[:, None], axis=2)
    own_norms = jnp.sum(across_u * member, axis=1)
    summed = lax.psum(own_norms, "section")
    example_norms = jnp.sqrt(summed)[:, None, :]
    clip_scale = jnp.minimum(1.0, clip_bound * lax.rsqrt(summed))
    token_scale = jnp.sum(member * clip_scale[:, None, :], axis=-1).reshape(tokens, 1)

    scaled_grad = (own_grad.astype(f32) * token_scale).astype(bf16)
    scaled_act = (own_act.astype(f32) * token_scale).astype(bf16)
    block = (NZ, NY) + own_down.shape
    part_down = mm("td,tk->dk", flat_in, scaled_grad).astype(bf16).reshape(block)
    part_up = mm("itd,tk->idk", loss_full, scaled_act).astype(bf16).reshape(block)
    cross_up = mm("stm,tn->smn", grads, scaled_act).reshape(sections * bottleneck, bottleneck)
    cross_up = sum_everywhere(cross_up).reshape(sections, bottleneck, bottleneck)
    cross_up = jnp.where(later, cross_up, 0)

    sum_down = scatter_z_then_y(part_down, z, y)
    sum_up = scatter_y_then_z(part_up, z, y) + mm("skm,smn->kn", down_rows, cross_up)
    new_down = run_down[0] + sum_down + noise_down[0]
    new_up = run_up[0] + sum_up + noise_up[0]
    return (new_down[None], new_up[None], example_norms)


def solution(mesh):
    return jax.shard_map(
        shards,
        mesh=mesh,
        in_specs=(
            P("section", None, "dp", None, None),
            P(None, "dp", None),
            P(None, "dp", None, "section"),
            P("section", "dp", None),
            P("section", "dp", None),
            P("section", "dp", None),
            P("section", "dp", None),
            P("section", "dp", None),
            P("section", "dp", None),
        ),
        out_specs=(P("section", "dp", None), P("section", "dp", None), P(None, "dp", None)),
        check_vma=False,
    )
```

```python
import jax
import jax.numpy as jnp
from jax import lax
from jax.experimental import pallas as pl
from jax.experimental.pallas import tpu as pltpu
from jax.sharding import PartitionSpec as P

EX = 2
NZ, NY = 8, 4
NX, NC = 4, 2

clip_bound = 400.0
bf16 = jnp.bfloat16
f32 = jnp.float32


def shift_z(value, d):
    pairs = [(z * NY + y, (z + d) % NZ * NY + y) for z in range(NZ) for y in range(NY)]
    return lax.ppermute(value, "dp", pairs)


def shift_y(value, d):
    pairs = [(z * NY + y, z * NY + (y + d) % NY) for z in range(NZ) for y in range(NY)]
    return lax.ppermute(value, "dp", pairs)


def shift_x(value, d):
    pairs = [(x * NC + c, (x + d) % NX * NC + c) for x in range(NX) for c in range(NC)]
    return lax.ppermute(value, "section", pairs)


def swap_core(value):
    return lax.ppermute(value, "section", [(s, s ^ 1) for s in range(NX * NC)])


def pick(value, index, axis=0):
    return lax.dynamic_index_in_dim(value, index, axis, keepdims=False)


def put(buffer, value, index, axis=0):
    return lax.dynamic_update_index_in_dim(buffer, value, index, axis)


def put_at(buffer, piece, first, second):
    return lax.dynamic_update_slice(buffer, piece[None, None], (first, second, 0, 0))


def together(*moves, also=()):
    moved = tuple(move(value, *by) for move, value, *by in moves)
    return lax.optimization_barrier(moved + tuple(also))


class At:
    def __init__(self, value):
        self.value = value

    def __add__(self, other):
        return At(lambda p: self.value(p) + number(other, p))

    def __sub__(self, other):
        return At(lambda p: self.value(p) - number(other, p))

    def __rsub__(self, other):
        return At(lambda p: number(other, p) - self.value(p))

    def __mul__(self, other):
        return At(lambda p: self.value(p) * number(other, p))

    def __mod__(self, other):
        return At(lambda p: lax.rem(self.value(p), jnp.int32(other)))

    __radd__, __rmul__ = (__add__, __mul__)


def number(value, p):
    return value.value(p) if isinstance(value, At) else value


AT_X, AT_CORE, AT_Z, AT_Y = (At(lambda p, k=k: p[k]) for k in range(4))


def row(value, p):
    return pl.multiple_of(value.value(p), 16) if isinstance(value, At) else value


class Operands:
    def __init__(self):
        self.arrays = []

    def array(self, value):
        for k, known in enumerate(self.arrays):
            if known is value:
                return k
        self.arrays.append(value)
        return len(self.arrays) - 1

    def call(self, kernel, out_shape, out_specs, scratch, flops=0, moved=0):
        section, place = (lax.axis_index("section"), lax.axis_index("dp"))
        here = jnp.stack([section // NC, section % NC, place // NY, place % NY]).astype(jnp.int32)
        def body(position, *refs):
            kernel([position[k] for k in range(4)], *refs)

        return pl.pallas_call(
            body,
            out_shape=out_shape,
            in_specs=[pl.BlockSpec(memory_space=pltpu.SMEM)]
            + [pl.BlockSpec(memory_space=pl.ANY)] * len(self.arrays),
            out_specs=out_specs,
            scratch_shapes=scratch,
            compiler_params=pltpu.CompilerParams(vmem_limit_bytes=57 << 20),
            cost_estimate=pl.CostEstimate(flops=flops, bytes_accessed=moved, transcendentals=0),
        )(here, *self.arrays)


def load(copies, sems, source, target):
    copies.append(pltpu.make_async_copy(source, target, sems.at[len(copies)]))
    copies[-1].start()


def pack(*jobs):
    held = Operands()
    plan = []
    for out, job in enumerate(jobs):
        low = 0
        for array, start, rows in job:
            plan.append((out, low, rows, held.array(array), start))
            low += rows
    shapes = [
        jax.ShapeDtypeStruct((sum(p[2] for p in job),) + job[0][0].shape[1:], job[0][0].dtype)
        for job in jobs
    ]
    count = len(held.arrays)

    def kernel(p, *refs):
        ins, outs = (refs[:count], refs[count : count + len(jobs)])
        buffers, (in_sems, out_sems) = (refs[count + len(jobs) : -2], refs[-2:])
        copies = []
        for out, low, rows, k, place in plan:
            source = ins[k].at[pl.ds(row(place, p), rows)]
            load(copies, in_sems, source, buffers[out].at[pl.ds(low, rows)])
        stores = []
        for out in range(len(jobs)):
            for copy, step in zip(copies, plan):
                if step[0] == out:
                    copy.wait()
            load(stores, out_sems, buffers[out], outs[out])
        for store in stores:
            store.wait()

    specs = [pl.BlockSpec(memory_space=pl.ANY)] * len(jobs)
    scratch = [pltpu.VMEM(t.shape, t.dtype) for t in shapes]
    scratch += [pltpu.SemaphoreType.DMA((len(plan),)), pltpu.SemaphoreType.DMA((len(jobs),))]
    moved = sum(2 * t.size * t.dtype.itemsize for t in shapes)
    return held.call(kernel, shapes, specs, scratch, 0, moved)


def assemble(pieces, total):
    held = Operands()
    plan = [(held.array(a), low, rows, at) for a, low, rows, at in pieces]
    shape = jax.ShapeDtypeStruct((total,) + pieces[0][0].shape[1:], pieces[0][0].dtype)
    count = len(held.arrays)

    def kernel(p, *refs):
        ins = refs[:count]
        whole, buffer, sems, out_sem = refs[count:]
        copies = []
        for k, low, rows, at in plan:
            source = ins[k].at[pl.ds(row(low, p), rows)]
            load(copies, sems, source, buffer.at[pl.ds(row(at, p), rows)])
        for copy in copies:
            copy.wait()
        store = pltpu.make_async_copy(buffer, whole, out_sem)
        store.start()
        store.wait()

    spec = pl.BlockSpec(memory_space=pl.ANY)
    scratch = [
        pltpu.VMEM(shape.shape, shape.dtype),
        pltpu.SemaphoreType.DMA((len(plan),)),
        pltpu.SemaphoreType.DMA,
    ]
    return held.call(kernel, shape, spec, scratch, 0, 2 * shape.size * shape.dtype.itemsize)


AROUND_X = (0, NX - 1, 1, 2)


def by_section(own, other, rows):
    pieces = []
    for k, d in enumerate(AROUND_X):
        place = (AT_X + d) % NX * NC
        pieces.append(own[k] + (rows, (place + AT_CORE) * rows))
        pieces.append(other[k] + (rows, (place + 1 - AT_CORE) * rows))
    return assemble(pieces, NX * NC * rows)


def section_gather(value, *also):
    before, after, across, mine, *also = together(
        (shift_x, value, 1), (shift_x, value, -1), (shift_x, value, 2), (swap_core, value), also=also
    )
    others = together((swap_core, before), (swap_core, after), (swap_core, across))
    own = [(v, 0) for v in (value, before, after, across)]
    return by_section(own, [(v, 0) for v in (mine,) + tuple(others)], value.shape[0]), *also


def fold(*jobs, dtype=bf16):
    held = Operands()
    plan, scratch, moved = ([], [], 0)
    for job in jobs:
        segments = []
        for rows, sources in job:
            names = []
            for array, start in sources:
                names.append((held.array(array), start, len(scratch)))
                scratch.append(pltpu.VMEM((rows, array.shape[1]), array.dtype))
                moved += rows * array.shape[1] * array.dtype.itemsize
            segments.append((rows, names))
        plan.append(segments)
    width = jobs[0][0][1][0][0].shape[1]
    shapes = [jax.ShapeDtypeStruct((sum(rows for rows, _ in job), width), dtype) for job in jobs]
    count, loads = (len(held.arrays), len(scratch))
    scratch = scratch + [pltpu.VMEM(t.shape, t.dtype) for t in shapes]
    scratch += [pltpu.SemaphoreType.DMA((loads,)), pltpu.SemaphoreType.DMA((len(jobs),))]

    def kernel(p, *refs):
        ins, outs = (refs[:count], refs[count : count + len(jobs)])
        buffers, results = (refs[count + len(jobs) :][:loads], refs[-2 - len(jobs) : -2])
        in_sems, out_sems = refs[-2:]
        copies = {}
        for segments in plan:
            for rows, names in segments:
                for k, place, n in names:
                    source = ins[k].at[pl.ds(row(place, p), rows)]
                    copies[n] = pltpu.make_async_copy(source, buffers[n], in_sems.at[n])
                    copies[n].start()
        stores = []
        for j, segments in enumerate(plan):
            low = 0
            for rows, names in segments:
                for _, _, n in names:
                    copies[n].wait()
                total = buffers[names[0][2]][...].astype(f32)
                for _, _, n in names[1:]:
                    total = total + buffers[n][...].astype(f32)
                results[j][low : low + rows, :] = total.astype(dtype)
                low += rows
            stores.append(pltpu.make_async_copy(results[j], outs[j], out_sems.at[j]))
            stores[-1].start()
        for store in stores:
            store.wait()

    specs = [pl.BlockSpec(memory_space=pl.ANY)] * len(jobs)
    return held.call(kernel, shapes, specs, scratch, 0, moved)


def gather_all(down, up, loss, beside):
    rows = down.shape[0]
    z, y = (AT_Z, AT_Y)
    none = (0, rows)

    q1, q3, q2, *_ = together((shift_y, down, 1), (shift_y, down, -1), (shift_y, down, 2))
    quad_ys = (0, -1, 1, 2)
    (m,) = pack([(v,) + none for v in (down, q1, q3, q2, up)])
    f1, b1, w1, w3, w2, *_ = together(
        (shift_z, m, 1),
        (shift_z, m, -1),
        (shift_x, down, 1),
        (shift_x, down, -1),
        (shift_x, down, 2),
        also=beside(1),
    )
    (down_x,) = pack([(v,) + none for v in (down, w1, w3, w2)])
    f2, b2, loss_1, loss_3, down_other, *_ = together(
        (shift_z, f1, 1), (shift_z, b1, -1), (shift_x, loss, 1), (shift_x, loss, -1), (swap_core, down_x)
    )
    last = NY * rows
    (near,) = pack([(up, 0, rows)] + [(v, last, rows) for v in (f1, b1, f2, b2)])
    down_rows = by_section(
        [(v, 0) for v in (down, w1, w3, w2)], [(down_other, k * rows) for k in range(NX)], rows
    )
    f3, b3, near_1, near_3, loss_2, *_ = together(
        (shift_z, f2, 1),
        (shift_z, b2, -1),
        (shift_y, near, 1),
        (shift_y, near, -1),
        (shift_x, loss_1, 1),
        also=beside(3, down_rows),
    )
    cut = near.shape[0] // 32 * 16
    near_low, near_high, f3_low, b3_high = pack(
        [(near_1, 0, cut)],
        [(near_3, cut, near.shape[0] - cut)],
        [(f3, k * rows, rows) for k in range(3)],
        [(b3, k * rows, rows) for k in range(3, 5)],
    )
    f4, b4, near_low, near_high, swap_0, swap_1, swap_3, *_ = together(
        (shift_z, f3_low, 1),
        (shift_z, b3_high, -1),
        (shift_y, near_low, 1),
        (shift_y, near_high, -1),
        (swap_core, loss),
        (swap_core, loss_1),
        (swap_core, loss_3),
        also=beside(4),
    )

    def where(dz, dy):
        return ((z + (NZ + dz)) % NZ * NY + (y + (NY + dy)) % NY) * rows

    downs = []
    for array, dz in ((m, 0), (f1, -1), (b1, 1), (f2, -2), (b2, 2), (f3, -3), (b3, 3)):
        downs += [(array, k * rows, rows, where(dz, dy)) for k, dy in enumerate(quad_ys)]
    downs += [(f4, k * rows, rows, where(4, quad_ys[k])) for k in range(3)]
    downs += [(b4, 0, rows, where(4, quad_ys[3]))]

    (far,) = pack([(f3, last, rows), (b3, last, rows), (b4, rows, rows)])
    far_1, far_3, swap_2, *_ = together(
        (shift_y, far, 1), (shift_y, far, -1), (swap_core, loss_2), also=beside(5, downs)
    )
    near_zs, far_zs = ((0, -1, 1, -2, 2), (-3, 3, 4))

    def quarter(dy):
        return (y + (NY + dy)) % NY * rows

    ups_near, ups_far = ([], [])
    for array, dy in ((near, 0), (near_1, -1), (near_3, 1)):
        ups_near += [(array, k * rows, rows, k * last + quarter(dy)) for k in range(5)]
    split = cut - 2 * rows
    ups_near += [(near_low, k * rows, rows, k * last + quarter(2)) for k in range(2)]
    ups_near += [(near_low, 2 * rows, split, 2 * last + quarter(2))]
    ups_near += [(near_high, 0, rows - split, 2 * last + quarter(2) + split)]
    ups_near += [
        (near_high, (k - 2) * rows - split, rows, k * last + quarter(2)) for k in range(3, 5)
    ]
    near_at = [(z + (NZ + dz)) % NZ for dz in near_zs]
    far_at = [(z + (NZ + dz)) % NZ for dz in far_zs]
    losses = []
    pieces = ((loss, swap_0), (loss_1, swap_1), (loss_3, swap_3), (loss_2, swap_2))
    for (piece, swapped), d in zip(pieces, AROUND_X):
        place = (AT_X + d) % NX * NC
        losses += [(piece, place + AT_CORE), (swapped, place + 1 - AT_CORE)]

    far_2, *done = together((shift_y, far_1, 1), also=beside(6, losses, ups_near, near_at))
    for array, dy in ((far, 0), (far_1, -1), (far_3, 1), (far_2, 2)):
        ups_far += [(array, k * rows, rows, k * last + quarter(dy)) for k in range(3)]
    return downs, (ups_far, far_at), done


def gelu_parts(hidden):
    normal_cdf = 0.5 * (1.0 + lax.erf(hidden * 0.7071067811865476))
    normal_pdf = jnp.exp(-0.5 * hidden * hidden) * 0.3989422804014327
    return (hidden * normal_cdf, normal_cdf + hidden * normal_pdf)


def project_inputs(inputs, downs):
    held = Operands()
    tokens, depth = inputs.shape
    width = downs[0][0].shape[1]
    n_in = held.array(inputs)
    plan = [(held.array(a), low, rows, at) for a, low, rows, at in downs]
    count = len(held.arrays)
    parts = 4
    chunk = depth // parts

    def kernel(p, *refs):
        ins = refs[:count]
        act, slope, xs, wd, sems = refs[count:]
        copies = []
        for k, low, rows, at in plan:
            load(copies, sems, ins[k].at[pl.ds(row(low, p), rows)], wd.at[pl.ds(row(at, p), rows)])
        for j in range(parts):
            load(copies, sems, ins[n_in].at[:, pl.ds(j * chunk, chunk)], xs.at[j])
        for copy in copies[: len(plan)]:
            copy.wait()
        value = jnp.zeros((tokens, width), f32)
        for j in range(parts):
            copies[len(plan) + j].wait()
            weights = wd[j * chunk : (j + 1) * chunk, :]
            value = value + jnp.dot(xs[j], weights, preferred_element_type=f32)
        gated, rise = gelu_parts(value)
        act[...] = gated.astype(bf16)
        slope[...] = rise.astype(bf16)

    shapes = [jax.ShapeDtypeStruct((tokens, width), bf16)] * 2
    scratch = [
        pltpu.VMEM((parts, tokens, chunk), bf16),
        pltpu.VMEM((depth, width), bf16),
        pltpu.SemaphoreType.DMA((len(plan) + parts,)),
    ]
    specs = [pl.BlockSpec(memory_space=pltpu.VMEM)] * 2
    return held.call(kernel, shapes, specs, scratch, 2 * tokens * depth * width, 9 << 20)


def project_near(losses, ups, at):
    held = Operands()
    tokens, slice_width = losses[0][0].shape
    width = ups[0][0].shape[1]
    loss_at = [(held.array(a), place) for a, place in losses]
    plan = [(held.array(a), low, rows, to) for a, low, rows, to in ups]
    count = len(held.arrays)
    n_loss = len(losses)

    def kernel(p, *refs):
        ins = refs[:count]
        out, whole, g, wu, sems, out_sem = refs[count:]
        copies = []
        for k, place in loss_at:
            load(copies, sems, ins[k], g.at[number(place, p)])
        for k, low, rows, to in plan:
            load(copies, sems, ins[k].at[pl.ds(row(low, p), rows)], wu.at[pl.ds(row(to, p), rows)])
        for copy in copies[:n_loss]:
            copy.wait()
        store = pltpu.make_async_copy(g, whole, out_sem)
        store.start()
        for copy in copies[n_loss:]:
            copy.wait()
        value = jnp.zeros((tokens, width), f32)
        for j in range(len(at)):
            weights = wu[j * slice_width : (j + 1) * slice_width, :]
            value = value + jnp.dot(g[number(at[j], p)], weights, preferred_element_type=f32)
        out[...] = value
        store.wait()

    shapes = [
        jax.ShapeDtypeStruct((tokens, width), f32),
        jax.ShapeDtypeStruct((n_loss, tokens, slice_width), bf16),
    ]
    scratch = [
        pltpu.VMEM(shapes[1].shape, bf16),
        pltpu.VMEM((len(at) * slice_width, width), bf16),
        pltpu.SemaphoreType.DMA((n_loss + len(plan),)),
        pltpu.SemaphoreType.DMA,
    ]
    specs = [pl.BlockSpec(memory_space=pltpu.VMEM), pl.BlockSpec(memory_space=pl.ANY)]
    return held.call(
        kernel, shapes, specs, scratch, 2 * tokens * len(at) * slice_width * width, 12 << 20
    )


def project_slices(start, loss_full, weights, at, dtype):
    held = Operands()
    _, tokens, slice_width = loss_full.shape
    width = weights[0][0].shape[1]
    n_loss, n_start = (held.array(loss_full), held.array(start))
    plan = [(held.array(a), low, rows, to) for a, low, rows, to in weights]
    count = len(held.arrays)
    slices = len(at)

    def kernel(p, *refs):
        ins = refs[:count]
        out, g, w, total, sems = refs[count:]
        copies = []
        load(copies, sems, ins[n_start], total)
        for j in range(slices):
            load(copies, sems, ins[n_loss].at[number(at[j], p)], g.at[j])
        for k, low, rows, to in plan:
            load(copies, sems, ins[k].at[pl.ds(row(low, p), rows)], w.at[pl.ds(row(to, p), rows)])
        for copy in copies:
            copy.wait()
        value = total[...]
        for j in range(slices):
            part = w[j * slice_width : (j + 1) * slice_width, :]
            value = value + jnp.dot(g[j], part, preferred_element_type=f32)
        out[...] = value.astype(dtype)

    shape = jax.ShapeDtypeStruct((tokens, width), dtype)
    scratch = [
        pltpu.VMEM((slices, tokens, slice_width), bf16),
        pltpu.VMEM((slices * slice_width, width), bf16),
        pltpu.VMEM((tokens, width), f32),
        pltpu.SemaphoreType.DMA((1 + slices + len(plan),)),
    ]
    spec = pl.BlockSpec(memory_space=pltpu.VMEM)
    moved = slices * slice_width * (tokens + width) * 2
    return held.call(kernel, shape, spec, scratch, 2 * tokens * slices * slice_width * width, moved)


def gradient_parts(inputs, loss_full, scaled_grad, scaled_act, firsts):
    held = Operands()
    tokens, depth = inputs.shape
    slices, _, slice_width = loss_full.shape
    width = scaled_grad.shape[1]
    n_in, n_loss = (held.array(inputs), held.array(loss_full))
    n_grad, n_act = (held.array(scaled_grad), held.array(scaled_act))
    plan = []
    for out, job in enumerate(firsts):
        low = 0
        for which, start, rows in job:
            plan.append((out, low, rows, which, start))
            low += rows
    count = len(held.arrays)
    parts = 4
    wide = depth // parts

    def kernel(p, *refs):
        ins, outs = (refs[:count], refs[count : count + 2 + len(firsts)])
        xs, g, sh, sa, pd, pu, in_sems, out_sems = refs[count + 2 + len(firsts) :]
        copies = []
        load(copies, in_sems, ins[n_act], sa)
        load(copies, in_sems, ins[n_grad], sh)
        for i in range(slices):
            load(copies, in_sems, ins[n_loss].at[i], g.at[i])
        for j in range(parts):
            span = pl.ds(j * wide, wide)
            load(copies, in_sems, ins[n_in].at[:, span], xs.at[:, span])
        stores = []
        over_tokens = (((0,), (0,)), ((), ()))
        copies[0].wait()
        copies[1].wait()
        act = sa[...]
        for i in range(slices):
            copies[2 + i].wait()
            span = pl.ds(i * slice_width, slice_width)
            part = lax.dot_general(g[i], act, over_tokens, preferred_element_type=f32)
            pu[span, :] = part.astype(bf16)
            load(stores, out_sems, pu.at[span], outs[1].at[span])
        grad = sh[...]
        for j in range(parts):
            copies[2 + slices + j].wait()

            def step(i, none):
                span = pl.ds(pl.multiple_of(j * wide + i * 128, 128), 128)
                part = lax.dot_general(xs[:, span], grad, over_tokens, preferred_element_type=f32)
                pd[span, :] = part.astype(bf16)
                return none

            lax.fori_loop(0, wide // 128, step, 0, unroll=True)
            span = pl.ds(j * wide, wide)
            load(stores, out_sems, pd.at[span], outs[0].at[span])
        for out, low, rows, which, place in plan:
            source = (pd, pu)[which].at[pl.ds(row(place, p), rows)]
            load(stores, out_sems, source, outs[2 + out].at[pl.ds(low, rows)])
        for store in stores:
            store.wait()

    shapes = [jax.ShapeDtypeStruct((depth, width), bf16)] * 2
    shapes += [jax.ShapeDtypeStruct((sum(p[2] for p in job), width), bf16) for job in firsts]
    scratch = [
        pltpu.VMEM((tokens, depth), bf16),
        pltpu.VMEM((slices, tokens, slice_width), bf16),
        pltpu.VMEM((tokens, width), bf16),
        pltpu.VMEM((tokens, width), bf16),
        pltpu.VMEM((depth, width), bf16),
        pltpu.VMEM((depth, width), bf16),
        pltpu.SemaphoreType.DMA((2 + slices + parts,)),
        pltpu.SemaphoreType.DMA((slices + parts + len(plan),)),
    ]
    specs = [pl.BlockSpec(memory_space=pl.ANY)] * len(shapes)
    return held.call(kernel, shapes, specs, scratch, 4 * tokens * depth * width, 17 << 20)


FAR, NEAR = ((3, -3, 4), (0, 1, -1, 2, -2))


def first_pieces(rows):
    z, y = (AT_Z, AT_Y)
    half = NY * rows // 2
    cut = len(FAR) * rows // 32 * 16
    opposite = (z + NZ // 2) % NZ * NY * rows
    blocks = [((z + (NZ + k)) % NZ * NY + (y + 2) % NY) * rows for k in FAR]
    split = cut - rows
    return (
        ((0, opposite, half),),
        ((0, opposite + half, half),),
        ((1, blocks[0], rows), (1, blocks[1], split)),
        ((1, blocks[1] + split, rows - split), (1, blocks[2], rows)),
    )


def scatter_all(pd, pu, firsts, rows, beside):
    z, y = (AT_Z, AT_Y)
    cut = rows // 32 * 16
    full = NY * rows
    half = full // 2
    far_cut = len(FAR) * rows // 32 * 16
    split = far_cut - rows

    def dz(k):
        return (z + (NZ + k)) % NZ * full

    def uz(k, d):
        return ((z + (NZ + k)) % NZ * NY + (y + (NY + d)) % NY) * rows

    f0, b0, u0, d0 = firsts
    f, b, u, d, *_ = together(
        (shift_z, f0, 1), (shift_z, b0, -1), (shift_y, u0, 1), (shift_y, d0, -1), also=beside(0)
    )
    rest = rows - split
    f, b, u, d = fold(
        [(half, [(pd, dz(3)), (f, 0)]), (half, [(pd, dz(3) + half)])],
        [(half, [(pd, dz(-3))]), (half, [(pd, dz(-3) + half), (b, 0)])],
        [
            (rows, [(pu, uz(FAR[0], 1)), (u, 0)]),
            (split, [(pu, uz(FAR[1], 1)), (u, rows)]),
            (rest, [(pu, uz(FAR[1], 1) + split)]),
            (rows, [(pu, uz(FAR[2], 1))]),
        ],
        [
            (rows, [(pu, uz(FAR[0], -1))]),
            (split, [(pu, uz(FAR[1], -1))]),
            (rest, [(pu, uz(FAR[1], -1) + split), (d, 0)]),
            (rows, [(pu, uz(FAR[2], -1)), (d, rest)]),
        ],
    )
    f, b, uf, df = together((shift_z, f, 1), (shift_z, b, -1), (shift_y, u, 1), (shift_y, d, -1))

    def far(k, low):
        return [(pu, uz(FAR[k], 0) + low), (uf, k * rows + low), (df, k * rows + low)]

    f, b, across = fold(
        [(full, [(pd, dz(2)), (f, 0)]), (cut, far(2, 0))],
        [(full, [(pd, dz(-2)), (b, 0)]), (rows - cut, far(2, cut))],
        [(rows, [(pu, uz(k, 2))]) for k in NEAR],
    )
    f, b, u = together((shift_z, f, 1), (shift_z, b, -1), (shift_y, across, 1))
    f, b, u, d = fold(
        [(full, [(pd, dz(1)), (f, 0)]), (cut, far(0, 0) + [(f, full)]), (rows - cut, far(0, cut))],
        [(full, [(pd, dz(-1)), (b, 0)]), (cut, far(1, 0)), (rows - cut, far(1, cut) + [(b, full)])],
        [(rows, [(pu, uz(k, 1)), (u, n * rows)]) for n, k in enumerate(NEAR)],
        [(rows, [(pu, uz(k, -1))]) for k in NEAR],
    )
    f, b, un, dn, *_ = together(
        (shift_z, f, 1), (shift_z, b, -1), (shift_y, u, 1), (shift_y, d, -1), also=beside(3)
    )

    def near(n):
        return [(pu, uz(NEAR[n], 0)), (un, n * rows), (dn, n * rows)]

    def own(d):
        low = (y + (NY + d)) % NY * rows
        return [(pd, dz(0) + low), (f, low), (b, low)]

    fz, bz, e1, e2, e3 = fold(
        [(rows, near(3) + [(f, full)])],
        [(rows, near(4) + [(b, full)])],
        [(rows, own(1))],
        [(rows, own(-1))],
        [(rows, own(2))],
    )
    fz, bz, e1, e2, e3, *_ = together(
        (shift_z, fz, 1),
        (shift_z, bz, -1),
        (shift_y, e1, 1),
        (shift_y, e2, -1),
        (shift_y, e3, 2),
        also=beside(4),
    )
    fz, bz = fold([(rows, near(1) + [(fz, 0)])], [(rows, near(2) + [(bz, 0)])])
    fz, bz, *done = together((shift_z, fz, 1), (shift_z, bz, -1), also=beside(5))
    return own(0) + [(e1, 0), (e2, 0), (e3, 0)], near(0) + [(fz, 0), (bz, 0)], done


def spread(parts):
    count = lax.axis_size("dp")
    rows, width = parts.shape
    split = parts.astype(bf16).reshape(count, rows // count, width)
    return lax.all_to_all(split, "dp", 0, 0)


def collect(arrived):
    summed = jnp.sum(arrived.astype(f32), axis=0).astype(bf16)
    sent = jnp.broadcast_to(summed[None], arrived.shape)
    return lax.all_to_all(sent, "dp", 0, 0).reshape(-1, arrived.shape[2])


def mm(subs, *operands):
    return jnp.einsum(subs, *operands, preferred_element_type=f32)


def shards(
    saved_inputs, example_ids, loss_grads, w_down, w_up, run_down, run_up, noise_down, noise_up
):
    sections = lax.axis_size("section")
    section = lax.axis_index("section")
    order = jnp.arange(sections)
    inputs = saved_inputs[0, :, 0]
    micro_count, tok_count, model_width = inputs.shape
    tokens = micro_count * tok_count
    bottleneck = w_down.shape[2]
    flat_in = inputs.reshape(tokens, model_width)
    loss_own = loss_grads[:, 0]
    slice_width = loss_own.shape[2]
    own_down, own_up = (w_down[0], w_up[0])

    later = (order > section)[:, None, None]
    work = {}

    def before_chain(turn, *given):
        if turn == 1:
            work["inputs"] = mm("btd,bud->btu", inputs, inputs)
            work["loss"] = mm("btd,bud->btu", loss_own, loss_own)
            return [work["inputs"], work["loss"]]
        if turn == 3:
            down_rows = given[0].reshape((sections,) + own_down.shape)
            cross = jnp.where(
                later, mm("skm,kn->smn", down_rows, own_up), mm("skm,kn->smn", down_rows, own_down)
            )
            work["down_rows"] = down_rows
            work["cross"] = cross.astype(bf16).reshape(sections * bottleneck, bottleneck)
            return [work["cross"]]
        if turn == 4:
            work["cross"] = spread(work["cross"])
            return [work["cross"]]
        if turn == 5:
            work["act"], work["slope"] = project_inputs(flat_in, *given)
            return [work["act"], work["slope"]]
        work["cross"] = collect(work["cross"])
        near = project_near(*given)
        return [work["act"], work["slope"], work["cross"], *near]

    downs, (ups_far, far_at), done = gather_all(
        own_down, own_up, loss_own.reshape(tokens, slice_width), before_chain
    )
    own_act, own_slope, cross, loss_up, loss_full = done
    loss_up = project_slices(loss_up, loss_full, ups_far, far_at, bf16)
    kept = cross.shape[0]
    (shared,) = pack([(cross, 0, kept)] + [(v, 0, tokens) for v in (own_act, own_slope, loss_up)])
    none = jnp.zeros((tokens, bottleneck), f32)
    loss_down = project_slices(none, loss_full, downs, list(range(sections)), f32)
    shared, loss_down = section_gather(shared, loss_down)
    shared = shared.reshape(sections, kept + 3 * tokens, bottleneck)
    cross = shared[:, :kept].reshape(sections, sections, bottleneck, bottleneck)
    shared = shared[:, kept:].reshape(sections, 3, tokens, bottleneck)
    acts, slopes, branch = (shared[:, 0], shared[:, 1], shared[:, 2].astype(f32))

    grads = [None] * sections
    for s in range(sections - 1, -1, -1):
        grads[s] = (branch[s] * slopes[s].astype(f32)).astype(bf16)
        if s:
            step = mm("tm,smn->stn", grads[s], cross[:s, s])
            branch = branch[:s] + step
    grads = jnp.stack(grads)
    own_grad, own_act = (pick(grads, section), pick(acts, section))

    weight = jnp.where(order > section, 1.0, jnp.where(order == section, 0.5, 0.0)).astype(bf16)
    mixed = mm("stn,smn->tm", grads * weight[:, None, None], pick(cross, section, 1))
    mixed = (loss_down + mixed).astype(bf16).reshape(micro_count, tok_count, bottleneck)
    grad_micro = own_grad.reshape(micro_count, tok_count, bottleneck)
    step_gram = mm("btk,buk->btu", mixed, grad_micro)
    step_gram = step_gram + jnp.swapaxes(step_gram, 1, 2)
    acts_micro = acts.reshape(sections, micro_count, tok_count, bottleneck)
    act_grams = mm("sbtk,sbuk->sbtu", acts_micro, acts_micro)
    before = (order < section).astype(f32)
    products = (
        work["inputs"] * mm("btk,buk->btu", grad_micro, grad_micro)
        + work["loss"] * jnp.sum(act_grams, axis=0)
        + step_gram * jnp.sum(act_grams * before[:, None, None, None], axis=0)
    )
    example_rows = example_ids[:, 0]
    member = (example_rows[:, :, None] == jnp.arange(EX, dtype=jnp.int32)).astype(f32)
    across_u = jnp.sum(products[..., None] * member[:, None], axis=2)
    own_norms = jnp.sum(across_u * member, axis=1)
    summed = lax.psum(own_norms, "section")
    example_norms = jnp.sqrt(summed)[:, None, :]
    clip_scale = jnp.minimum(1.0, clip_bound * lax.rsqrt(summed))
    token_scale = jnp.sum(member * clip_scale[:, None, :], axis=-1).reshape(tokens, 1)

    scaled_grad = (own_grad.astype(f32) * token_scale).astype(bf16)
    scaled_act = (own_act.astype(f32) * token_scale).astype(bf16)
    rows = own_down.shape[0]
    part_down, part_up, *firsts = gradient_parts(
        flat_in, loss_full, scaled_grad, scaled_act, first_pieces(rows)
    )

    def after_clip(turn):
        if turn == 0:
            cross_up = mm("stm,tn->smn", grads, scaled_act)
            cross_up = jnp.where(later, cross_up, 0).astype(bf16)
            work["up"] = cross_up.reshape(sections * bottleneck, bottleneck)
        if turn == 3:
            work["up"] = spread(work["up"])
        if turn == 5:
            work["up"] = collect(work["up"])
        return [work["up"]]

    downs, ups, (cross_up,) = scatter_all(part_down, part_up, firsts, rows, after_clip)
    cross_up = cross_up.reshape(sections, bottleneck, bottleneck)
    step_up = mm("skm,smn->kn", work["down_rows"], cross_up)
    new_down, new_up = fold(
        [(rows, downs + [(run_down[0], 0), (noise_down[0], 0)])],
        [(rows, ups + [(step_up, 0), (run_up[0], 0), (noise_up[0], 0)])],
        dtype=f32,
    )
    return (new_down[None], new_up[None], example_norms)


def solution(mesh):
    return jax.shard_map(
        shards,
        mesh=mesh,
        in_specs=(
            P("section", None, "dp", None, None),
            P(None, "dp", None),
            P(None, "dp", None, "section"),
            P("section", "dp", None),
            P("section", "dp", None),
            P("section", "dp", None),
            P("section", "dp", None),
            P("section", "dp", None),
            P("section", "dp", None),
        ),
        out_specs=(P("section", "dp", None), P("section", "dp", None), P(None, "dp", None)),
        check_vma=False,
    )
```

```python
import jax
import jax.numpy as jnp
from jax import lax
from jax.experimental import pallas as pl
from jax.experimental.pallas import tpu as pltpu
from jax.sharding import PartitionSpec as P

EX = 2
NZ, NY = 8, 4
NX, NC = 4, 2

clip_bound = 400.0
bf16 = jnp.bfloat16
f32 = jnp.float32


def shift_z(value, d):
    pairs = [(z * NY + y, (z + d) % NZ * NY + y) for z in range(NZ) for y in range(NY)]
    return lax.ppermute(value, "dp", pairs)


def shift_y(value, d):
    pairs = [(z * NY + y, z * NY + (y + d) % NY) for z in range(NZ) for y in range(NY)]
    return lax.ppermute(value, "dp", pairs)


def shift_x(value, d):
    pairs = [(x * NC + c, (x + d) % NX * NC + c) for x in range(NX) for c in range(NC)]
    return lax.ppermute(value, "section", pairs)


def swap_core(value):
    return lax.ppermute(value, "section", [(s, s ^ 1) for s in range(NX * NC)])


def pick(value, index, axis=0):
    return lax.dynamic_index_in_dim(value, index, axis, keepdims=False)


def put(buffer, value, index, axis=0):
    return lax.dynamic_update_index_in_dim(buffer, value, index, axis)


def put_at(buffer, piece, first, second):
    return lax.dynamic_update_slice(buffer, piece[None, None], (first, second, 0, 0))


def together(*moves, also=()):
    moved = tuple(move(value, *by) for move, value, *by in moves)
    return lax.optimization_barrier(moved + tuple(also))


class At:
    def __init__(self, value):
        self.value = value

    def __add__(self, other):
        return At(lambda p: self.value(p) + number(other, p))

    def __sub__(self, other):
        return At(lambda p: self.value(p) - number(other, p))

    def __rsub__(self, other):
        return At(lambda p: number(other, p) - self.value(p))

    def __mul__(self, other):
        return At(lambda p: self.value(p) * number(other, p))

    def __mod__(self, other):
        return At(lambda p: lax.rem(self.value(p), jnp.int32(other)))

    __radd__, __rmul__ = (__add__, __mul__)


def number(value, p):
    return value.value(p) if isinstance(value, At) else value


AT_X, AT_CORE, AT_Z, AT_Y = (At(lambda p, k=k: p[k]) for k in range(4))


def row(value, p):
    return pl.multiple_of(value.value(p), 16) if isinstance(value, At) else value


class Operands:
    def __init__(self):
        self.arrays = []

    def array(self, value):
        for k, known in enumerate(self.arrays):
            if known is value:
                return k
        self.arrays.append(value)
        return len(self.arrays) - 1

    def call(self, kernel, out_shape, out_specs, scratch, flops=0, moved=0, limit=57):
        section, place = (lax.axis_index("section"), lax.axis_index("dp"))
        here = jnp.stack([section // NC, section % NC, place // NY, place % NY]).astype(jnp.int32)
        def body(position, *refs):
            kernel([position[k] for k in range(4)], *refs)

        return pl.pallas_call(
            body,
            out_shape=out_shape,
            in_specs=[pl.BlockSpec(memory_space=pltpu.SMEM)]
            + [pl.BlockSpec(memory_space=pl.ANY)] * len(self.arrays),
            out_specs=out_specs,
            scratch_shapes=scratch,
            compiler_params=pltpu.CompilerParams(vmem_limit_bytes=limit << 20),
            cost_estimate=pl.CostEstimate(flops=flops, bytes_accessed=moved, transcendentals=0),
        )(here, *self.arrays)


def load(copies, sems, source, target):
    copies.append(pltpu.make_async_copy(source, target, sems.at[len(copies)]))
    copies[-1].start()


def pack(*jobs):
    held = Operands()
    plan = []
    for out, job in enumerate(jobs):
        low = 0
        for array, start, rows in job:
            plan.append((out, low, rows, held.array(array), start))
            low += rows
    shapes = [
        jax.ShapeDtypeStruct((sum(p[2] for p in job),) + job[0][0].shape[1:], job[0][0].dtype)
        for job in jobs
    ]
    count = len(held.arrays)

    def kernel(p, *refs):
        ins, outs = (refs[:count], refs[count : count + len(jobs)])
        buffers, (in_sems, out_sems) = (refs[count + len(jobs) : -2], refs[-2:])
        copies = []
        for out, low, rows, k, place in plan:
            source = ins[k].at[pl.ds(row(place, p), rows)]
            load(copies, in_sems, source, buffers[out].at[pl.ds(low, rows)])
        stores = []
        for out in range(len(jobs)):
            for copy, step in zip(copies, plan):
                if step[0] == out:
                    copy.wait()
            load(stores, out_sems, buffers[out], outs[out])
        for store in stores:
            store.wait()

    specs = [pl.BlockSpec(memory_space=pl.ANY)] * len(jobs)
    scratch = [pltpu.VMEM(t.shape, t.dtype) for t in shapes]
    scratch += [pltpu.SemaphoreType.DMA((len(plan),)), pltpu.SemaphoreType.DMA((len(jobs),))]
    moved = sum(2 * t.size * t.dtype.itemsize for t in shapes)
    return held.call(kernel, shapes, specs, scratch, 0, moved, 16)


def assemble(pieces, total):
    held = Operands()
    plan = [(held.array(a), low, rows, at) for a, low, rows, at in pieces]
    shape = jax.ShapeDtypeStruct((total,) + pieces[0][0].shape[1:], pieces[0][0].dtype)
    count = len(held.arrays)

    def kernel(p, *refs):
        ins = refs[:count]
        whole, buffer, sems, out_sem = refs[count:]
        copies = []
        for k, low, rows, at in plan:
            source = ins[k].at[pl.ds(row(low, p), rows)]
            load(copies, sems, source, buffer.at[pl.ds(row(at, p), rows)])
        for copy in copies:
            copy.wait()
        store = pltpu.make_async_copy(buffer, whole, out_sem)
        store.start()
        store.wait()

    spec = pl.BlockSpec(memory_space=pl.ANY)
    scratch = [
        pltpu.VMEM(shape.shape, shape.dtype),
        pltpu.SemaphoreType.DMA((len(plan),)),
        pltpu.SemaphoreType.DMA,
    ]
    return held.call(kernel, shape, spec, scratch, 0, 2 * shape.size * shape.dtype.itemsize, 16)


AROUND_X = (0, NX - 1, 1, 2)


def by_section(own, other, rows):
    pieces = []
    for k, d in enumerate(AROUND_X):
        place = (AT_X + d) % NX * NC
        pieces.append(own[k] + (rows, (place + AT_CORE) * rows))
        pieces.append(other[k] + (rows, (place + 1 - AT_CORE) * rows))
    return assemble(pieces, NX * NC * rows)


def section_gather(value, *also):
    before, after, across, mine, *also = together(
        (shift_x, value, 1), (shift_x, value, -1), (shift_x, value, 2), (swap_core, value), also=also
    )
    others = together((swap_core, before), (swap_core, after), (swap_core, across))
    own = [(v, 0) for v in (value, before, after, across)]
    return by_section(own, [(v, 0) for v in (mine,) + tuple(others)], value.shape[0]), *also


def fold(*jobs, dtype=bf16):
    held = Operands()
    plan, scratch, moved = ([], [], 0)
    for job in jobs:
        segments = []
        for rows, sources in job:
            names = []
            for array, start in sources:
                names.append((held.array(array), start, len(scratch)))
                scratch.append(pltpu.VMEM((rows, array.shape[1]), array.dtype))
                moved += rows * array.shape[1] * array.dtype.itemsize
            segments.append((rows, names))
        plan.append(segments)
    width = jobs[0][0][1][0][0].shape[1]
    shapes = [jax.ShapeDtypeStruct((sum(rows for rows, _ in job), width), dtype) for job in jobs]
    count, loads = (len(held.arrays), len(scratch))
    scratch = scratch + [pltpu.VMEM(t.shape, t.dtype) for t in shapes]
    scratch += [pltpu.SemaphoreType.DMA((loads,)), pltpu.SemaphoreType.DMA((len(jobs),))]

    def kernel(p, *refs):
        ins, outs = (refs[:count], refs[count : count + len(jobs)])
        buffers, results = (refs[count + len(jobs) :][:loads], refs[-2 - len(jobs) : -2])
        in_sems, out_sems = refs[-2:]
        copies = {}
        for segments in plan:
            for rows, names in segments:
                for k, place, n in names:
                    source = ins[k].at[pl.ds(row(place, p), rows)]
                    copies[n] = pltpu.make_async_copy(source, buffers[n], in_sems.at[n])
                    copies[n].start()
        stores = []
        for j, segments in enumerate(plan):
            low = 0
            for rows, names in segments:
                for _, _, n in names:
                    copies[n].wait()
                total = buffers[names[0][2]][...].astype(f32)
                for _, _, n in names[1:]:
                    total = total + buffers[n][...].astype(f32)
                results[j][low : low + rows, :] = total.astype(dtype)
                low += rows
            stores.append(pltpu.make_async_copy(results[j], outs[j], out_sems.at[j]))
            stores[-1].start()
        for store in stores:
            store.wait()

    specs = [pl.BlockSpec(memory_space=pl.ANY)] * len(jobs)
    return held.call(kernel, shapes, specs, scratch, 0, moved)


def gather_all(down, up, loss, beside):
    rows = down.shape[0]
    z, y = (AT_Z, AT_Y)
    none = (0, rows)

    q1, q3, q2, *_ = together((shift_y, down, 1), (shift_y, down, -1), (shift_y, down, 2))
    quad_ys = (0, -1, 1, 2)
    (m,) = pack([(v,) + none for v in (down, q1, q3, q2, up)])
    f1, b1, w1, w3, w2 = together(
        (shift_z, m, 1),
        (shift_z, m, -1),
        (shift_x, down, 1),
        (shift_x, down, -1),
        (shift_x, down, 2),
    )
    (down_x,) = pack([(v,) + none for v in (down, w1, w3, w2)])
    f2, b2, loss_1, loss_3, down_other, *_ = together(
        (shift_z, f1, 1), (shift_z, b1, -1), (shift_x, loss, 1), (shift_x, loss, -1), (swap_core, down_x)
    )
    last = NY * rows
    (near,) = pack([(up, 0, rows)] + [(v, last, rows) for v in (f1, b1, f2, b2)])
    down_rows = by_section(
        [(v, 0) for v in (down, w1, w3, w2)], [(down_other, k * rows) for k in range(NX)], rows
    )
    f3, b3, near_1, near_3, loss_2, *_ = together(
        (shift_z, f2, 1),
        (shift_z, b2, -1),
        (shift_y, near, 1),
        (shift_y, near, -1),
        (shift_x, loss_1, 1),
        also=beside(3, down_rows),
    )
    cut = near.shape[0] // 32 * 16
    near_low, near_high, f3_low, b3_high = pack(
        [(near_1, 0, cut)],
        [(near_3, cut, near.shape[0] - cut)],
        [(f3, k * rows, rows) for k in range(3)],
        [(b3, k * rows, rows) for k in range(3, 5)],
    )
    f4, b4, near_low, near_high, swap_0, swap_1, swap_3, *_ = together(
        (shift_z, f3_low, 1),
        (shift_z, b3_high, -1),
        (shift_y, near_low, 1),
        (shift_y, near_high, -1),
        (swap_core, loss),
        (swap_core, loss_1),
        (swap_core, loss_3),
        also=beside(4),
    )

    def where(dz, dy):
        return ((z + (NZ + dz)) % NZ * NY + (y + (NY + dy)) % NY) * rows

    downs = []
    for array, dz in ((m, 0), (f1, -1), (b1, 1), (f2, -2), (b2, 2), (f3, -3), (b3, 3)):
        downs += [(array, k * rows, rows, where(dz, dy)) for k, dy in enumerate(quad_ys)]
    downs += [(f4, k * rows, rows, where(4, quad_ys[k])) for k in range(3)]
    downs += [(b4, 0, rows, where(4, quad_ys[3]))]

    (far,) = pack([(f3, last, rows), (b3, last, rows), (b4, rows, rows)])
    far_1, far_3, swap_2, *_ = together(
        (shift_y, far, 1), (shift_y, far, -1), (swap_core, loss_2), also=beside(5, downs)
    )
    near_zs, far_zs = ((0, -1, 1, -2, 2), (-3, 3, 4))

    def quarter(dy):
        return (y + (NY + dy)) % NY * rows

    ups_near, ups_far = ([], [])
    for array, dy in ((near, 0), (near_1, -1), (near_3, 1)):
        ups_near += [(array, k * rows, rows, k * last + quarter(dy)) for k in range(5)]
    split = cut - 2 * rows
    ups_near += [(near_low, k * rows, rows, k * last + quarter(2)) for k in range(2)]
    ups_near += [(near_low, 2 * rows, split, 2 * last + quarter(2))]
    ups_near += [(near_high, 0, rows - split, 2 * last + quarter(2) + split)]
    ups_near += [
        (near_high, (k - 2) * rows - split, rows, k * last + quarter(2)) for k in range(3, 5)
    ]
    near_at = [(z + (NZ + dz)) % NZ for dz in near_zs]
    far_at = [(z + (NZ + dz)) % NZ for dz in far_zs]
    losses = []
    pieces = ((loss, swap_0), (loss_1, swap_1), (loss_3, swap_3), (loss_2, swap_2))
    for (piece, swapped), d in zip(pieces, AROUND_X):
        place = (AT_X + d) % NX * NC
        losses += [(piece, place + AT_CORE), (swapped, place + 1 - AT_CORE)]

    far_2, *done = together((shift_y, far_1, 1), also=beside(6, losses, ups_near, near_at))
    for array, dy in ((far, 0), (far_1, -1), (far_3, 1), (far_2, 2)):
        ups_far += [(array, k * rows, rows, k * last + quarter(dy)) for k in range(3)]
    return downs, (ups_far, far_at), done


def gelu_parts(hidden):
    normal_cdf = 0.5 * (1.0 + lax.erf(hidden * 0.7071067811865476))
    normal_pdf = jnp.exp(-0.5 * hidden * hidden) * 0.3989422804014327
    return (hidden * normal_cdf, normal_cdf + hidden * normal_pdf)


def project_inputs(inputs, downs):
    held = Operands()
    tokens, depth = inputs.shape
    width = downs[0][0].shape[1]
    n_in = held.array(inputs)
    plan = [(held.array(a), low, rows, at) for a, low, rows, at in downs]
    count = len(held.arrays)
    parts = 4
    chunk = depth // parts

    def kernel(p, *refs):
        ins = refs[:count]
        act, slope, xs, wd, sems = refs[count:]
        copies = []
        for k, low, rows, at in plan:
            load(copies, sems, ins[k].at[pl.ds(row(low, p), rows)], wd.at[pl.ds(row(at, p), rows)])
        for j in range(parts):
            load(copies, sems, ins[n_in].at[:, pl.ds(j * chunk, chunk)], xs.at[j])
        for copy in copies[: len(plan)]:
            copy.wait()
        value = jnp.zeros((tokens, width), f32)
        for j in range(parts):
            copies[len(plan) + j].wait()
            weights = wd[j * chunk : (j + 1) * chunk, :]
            value = value + jnp.dot(xs[j], weights, preferred_element_type=f32)
        gated, rise = gelu_parts(value)
        act[...] = gated.astype(bf16)
        slope[...] = rise.astype(bf16)

    shapes = [jax.ShapeDtypeStruct((tokens, width), bf16)] * 2
    scratch = [
        pltpu.VMEM((parts, tokens, chunk), bf16),
        pltpu.VMEM((depth, width), bf16),
        pltpu.SemaphoreType.DMA((len(plan) + parts,)),
    ]
    specs = [pl.BlockSpec(memory_space=pltpu.VMEM)] * 2
    return held.call(kernel, shapes, specs, scratch, 2 * tokens * depth * width, 9 << 20)


def project_near(losses, ups, at):
    held = Operands()
    tokens, slice_width = losses[0][0].shape
    width = ups[0][0].shape[1]
    loss_at = [(held.array(a), place) for a, place in losses]
    plan = [(held.array(a), low, rows, to) for a, low, rows, to in ups]
    count = len(held.arrays)
    n_loss = len(losses)

    def kernel(p, *refs):
        ins = refs[:count]
        out, whole, g, wu, sems, out_sem = refs[count:]
        copies = []
        for k, place in loss_at:
            load(copies, sems, ins[k], g.at[number(place, p)])
        for k, low, rows, to in plan:
            load(copies, sems, ins[k].at[pl.ds(row(low, p), rows)], wu.at[pl.ds(row(to, p), rows)])
        for copy in copies[:n_loss]:
            copy.wait()
        store = pltpu.make_async_copy(g, whole, out_sem)
        store.start()
        for copy in copies[n_loss:]:
            copy.wait()
        value = jnp.zeros((tokens, width), f32)
        for j in range(len(at)):
            weights = wu[j * slice_width : (j + 1) * slice_width, :]
            value = value + jnp.dot(g[number(at[j], p)], weights, preferred_element_type=f32)
        out[...] = value
        store.wait()

    shapes = [
        jax.ShapeDtypeStruct((tokens, width), f32),
        jax.ShapeDtypeStruct((n_loss, tokens, slice_width), bf16),
    ]
    scratch = [
        pltpu.VMEM(shapes[1].shape, bf16),
        pltpu.VMEM((len(at) * slice_width, width), bf16),
        pltpu.SemaphoreType.DMA((n_loss + len(plan),)),
        pltpu.SemaphoreType.DMA,
    ]
    specs = [pl.BlockSpec(memory_space=pltpu.VMEM), pl.BlockSpec(memory_space=pl.ANY)]
    return held.call(
        kernel, shapes, specs, scratch, 2 * tokens * len(at) * slice_width * width, 12 << 20
    )


def project_slices(start, loss_full, weights, at, dtype):
    held = Operands()
    _, tokens, slice_width = loss_full.shape
    width = weights[0][0].shape[1]
    n_loss, n_start = (held.array(loss_full), held.array(start))
    plan = [(held.array(a), low, rows, to) for a, low, rows, to in weights]
    count = len(held.arrays)
    slices = len(at)

    def kernel(p, *refs):
        ins = refs[:count]
        out, g, w, total, sems = refs[count:]
        copies = []
        load(copies, sems, ins[n_start], total)
        for j in range(slices):
            load(copies, sems, ins[n_loss].at[number(at[j], p)], g.at[j])
        for k, low, rows, to in plan:
            load(copies, sems, ins[k].at[pl.ds(row(low, p), rows)], w.at[pl.ds(row(to, p), rows)])
        for copy in copies:
            copy.wait()
        value = total[...]
        for j in range(slices):
            part = w[j * slice_width : (j + 1) * slice_width, :]
            value = value + jnp.dot(g[j], part, preferred_element_type=f32)
        out[...] = value.astype(dtype)

    shape = jax.ShapeDtypeStruct((tokens, width), dtype)
    scratch = [
        pltpu.VMEM((slices, tokens, slice_width), bf16),
        pltpu.VMEM((slices * slice_width, width), bf16),
        pltpu.VMEM((tokens, width), f32),
        pltpu.SemaphoreType.DMA((1 + slices + len(plan),)),
    ]
    spec = pl.BlockSpec(memory_space=pltpu.VMEM)
    moved = slices * slice_width * (tokens + width) * 2
    return held.call(kernel, shape, spec, scratch, 2 * tokens * slices * slice_width * width, moved)


def gradient_part(values, scaled, firsts):
    held = Operands()
    tokens, width = scaled.shape
    depth = values.size // tokens
    sliced = values.ndim == 3
    parts = values.shape[0] if sliced else 4
    wide = depth // parts
    n_values, n_scaled = (held.array(values), held.array(scaled))
    plan = []
    for out, job in enumerate(firsts):
        low = 0
        for start, rows in job:
            plan.append((out, low, rows, start))
            low += rows
    count = len(held.arrays)

    def kernel(p, *refs):
        ins, outs = (refs[:count], refs[count : count + 1 + len(firsts)])
        xs, sh, whole, in_sems, out_sems = refs[count + 1 + len(firsts) :]
        copies = []
        load(copies, in_sems, ins[n_scaled], sh)
        for j in range(parts):
            source = ins[n_values].at[j] if sliced else ins[n_values].at[:, pl.ds(j * wide, wide)]
            load(copies, in_sems, source, xs.at[j])
        stores = []
        over_tokens = (((0,), (0,)), ((), ()))
        copies[0].wait()
        factor = sh[...]
        for j in range(parts):
            copies[1 + j].wait()
            part = lax.dot_general(xs[j], factor, over_tokens, preferred_element_type=f32)
            span = pl.ds(j * wide, wide)
            whole[span, :] = part.astype(bf16)
            load(stores, out_sems, whole.at[span], outs[0].at[span])
        for out, low, rows, place in plan:
            source = whole.at[pl.ds(row(place, p), rows)]
            load(stores, out_sems, source, outs[1 + out].at[pl.ds(low, rows)])
        for store in stores:
            store.wait()

    shapes = [jax.ShapeDtypeStruct((depth, width), bf16)]
    shapes += [jax.ShapeDtypeStruct((sum(q[1] for q in job), width), bf16) for job in firsts]
    scratch = [
        pltpu.VMEM((parts, tokens, wide), bf16),
        pltpu.VMEM((tokens, width), bf16),
        pltpu.VMEM((depth, width), bf16),
        pltpu.SemaphoreType.DMA((1 + parts,)),
        pltpu.SemaphoreType.DMA((parts + len(plan),)),
    ]
    specs = [pl.BlockSpec(memory_space=pl.ANY)] * len(shapes)
    return held.call(kernel, shapes, specs, scratch, 2 * tokens * depth * width, 9 << 20)


FAR, NEAR = ((3, -3, 4), (0, 1, -1, 2, -2))


def first_pieces(rows):
    z, y = (AT_Z, AT_Y)
    half = NY * rows // 2
    cut = len(FAR) * rows // 32 * 16
    opposite = (z + NZ // 2) % NZ * NY * rows
    blocks = [((z + (NZ + k)) % NZ * NY + (y + 2) % NY) * rows for k in FAR]
    split = cut - rows
    return (
        (((opposite, half),), ((opposite + half, half),)),
        (
            ((blocks[0], rows), (blocks[1], split)),
            ((blocks[1] + split, rows - split), (blocks[2], rows)),
        ),
    )


def scatter_all(pd, pu, firsts, rows, beside):
    z, y = (AT_Z, AT_Y)
    cut = rows // 32 * 16
    full = NY * rows
    half = full // 2
    far_cut = len(FAR) * rows // 32 * 16
    split = far_cut - rows

    def dz(k):
        return (z + (NZ + k)) % NZ * full

    def uz(k, d):
        return ((z + (NZ + k)) % NZ * NY + (y + (NY + d)) % NY) * rows

    f0, b0, u0, d0 = firsts
    rest = rows - split
    f, b, *_ = together((shift_z, f0, 1), (shift_z, b0, -1))
    u, d, *_ = together((shift_y, u0, 1), (shift_y, d0, -1))
    f, b = fold(
        [(half, [(pd, dz(3)), (f, 0)]), (half, [(pd, dz(3) + half)])],
        [(half, [(pd, dz(-3))]), (half, [(pd, dz(-3) + half), (b, 0)])],
    )
    f, b, *_ = together((shift_z, f, 1), (shift_z, b, -1))
    u, d, across = fold(
        [
            (rows, [(pu, uz(FAR[0], 1)), (u, 0)]),
            (split, [(pu, uz(FAR[1], 1)), (u, rows)]),
            (rest, [(pu, uz(FAR[1], 1) + split)]),
            (rows, [(pu, uz(FAR[2], 1))]),
        ],
        [
            (rows, [(pu, uz(FAR[0], -1))]),
            (split, [(pu, uz(FAR[1], -1))]),
            (rest, [(pu, uz(FAR[1], -1) + split), (d, 0)]),
            (rows, [(pu, uz(FAR[2], -1)), (d, rest)]),
        ],
        [(rows, [(pu, uz(k, 2))]) for k in NEAR],
    )
    uf, df, *_ = together((shift_y, u, 1), (shift_y, d, -1), also=beside(0))

    def far(k, low):
        return [(pu, uz(FAR[k], 0) + low), (uf, k * rows + low), (df, k * rows + low)]

    f, b = fold(
        [(full, [(pd, dz(2)), (f, 0)]), (cut, far(2, 0))],
        [(full, [(pd, dz(-2)), (b, 0)]), (rows - cut, far(2, cut))],
    )
    (u,) = together((shift_y, across, 1))
    f, b, *_ = together((shift_z, f, 1), (shift_z, b, -1), also=beside(2))
    u, d = fold(
        [(rows, [(pu, uz(k, 1)), (u, n * rows)]) for n, k in enumerate(NEAR)],
        [(rows, [(pu, uz(k, -1))]) for k in NEAR],
    )
    un, dn, *_ = together((shift_y, u, 1), (shift_y, d, -1), also=beside(3))
    f, b = fold(
        [(full, [(pd, dz(1)), (f, 0)]), (cut, far(0, 0) + [(f, full)]), (rows - cut, far(0, cut))],
        [(full, [(pd, dz(-1)), (b, 0)]), (cut, far(1, 0)), (rows - cut, far(1, cut) + [(b, full)])],
    )
    f, b, *_ = together((shift_z, f, 1), (shift_z, b, -1))

    def near(n):
        return [(pu, uz(NEAR[n], 0)), (un, n * rows), (dn, n * rows)]

    def own(d):
        low = (y + (NY + d)) % NY * rows
        return [(pd, dz(0) + low), (f, low), (b, low)]

    fz, bz, e1, e2, e3 = fold(
        [(rows, near(3) + [(f, full)])],
        [(rows, near(4) + [(b, full)])],
        [(rows, own(1))],
        [(rows, own(-1))],
        [(rows, own(2))],
    )
    fz, bz = together((shift_z, fz, 1), (shift_z, bz, -1))
    e1, e2, e3 = together((shift_y, e1, 1), (shift_y, e2, -1), (shift_y, e3, 2))
    fz, bz = fold([(rows, near(1) + [(fz, 0)])], [(rows, near(2) + [(bz, 0)])])
    fz, bz, *done = together((shift_z, fz, 1), (shift_z, bz, -1), also=beside(5))
    return own(0) + [(e1, 0), (e2, 0), (e3, 0)], near(0) + [(fz, 0), (bz, 0)], done


def spread(parts):
    count = lax.axis_size("dp")
    rows, width = parts.shape
    split = parts.astype(bf16).reshape(count, rows // count, width)
    return lax.all_to_all(split, "dp", 0, 0)


def collect(arrived):
    summed = jnp.sum(arrived.astype(f32), axis=0).astype(bf16)
    sent = jnp.broadcast_to(summed[None], arrived.shape)
    return lax.all_to_all(sent, "dp", 0, 0).reshape(-1, arrived.shape[2])


def mm(subs, *operands):
    return jnp.einsum(subs, *operands, preferred_element_type=f32)


def shards(
    saved_inputs, example_ids, loss_grads, w_down, w_up, run_down, run_up, noise_down, noise_up
):
    sections = lax.axis_size("section")
    section = lax.axis_index("section")
    order = jnp.arange(sections)
    inputs = saved_inputs[0, :, 0]
    micro_count, tok_count, model_width = inputs.shape
    tokens = micro_count * tok_count
    bottleneck = w_down.shape[2]
    flat_in = inputs.reshape(tokens, model_width)
    loss_own = loss_grads[:, 0]
    slice_width = loss_own.shape[2]
    own_down, own_up = (w_down[0], w_up[0])

    later = (order > section)[:, None, None]
    work = {}

    def before_chain(turn, *given):
        if turn == 3:
            down_rows = given[0].reshape((sections,) + own_down.shape)
            cross = jnp.where(
                later, mm("skm,kn->smn", down_rows, own_up), mm("skm,kn->smn", down_rows, own_down)
            )
            work["down_rows"] = down_rows
            work["cross"] = cross.astype(bf16).reshape(sections * bottleneck, bottleneck)
            return [work["cross"]]
        if turn == 4:
            work["cross"] = spread(work["cross"])
            return [work["cross"]]
        if turn == 5:
            work["act"], work["slope"] = project_inputs(flat_in, *given)
            return [work["act"], work["slope"]]
        work["cross"] = collect(work["cross"])
        near = project_near(*given)
        return [work["act"], work["slope"], work["cross"], *near]

    downs, (ups_far, far_at), done = gather_all(
        own_down, own_up, loss_own.reshape(tokens, slice_width), before_chain
    )
    own_act, own_slope, cross, loss_up, loss_full = done
    loss_up = project_slices(loss_up, loss_full, ups_far, far_at, bf16)
    kept = cross.shape[0]
    (shared,) = pack([(cross, 0, kept)] + [(v, 0, tokens) for v in (own_act, own_slope, loss_up)])
    none = jnp.zeros((tokens, bottleneck), f32)
    loss_down = project_slices(none, loss_full, downs, list(range(sections)), f32)
    gram_in, gram_loss = (mm("btd,bud->btu", v, v) for v in (inputs, loss_own))
    shared, loss_down, gram_in, gram_loss = section_gather(shared, loss_down, gram_in, gram_loss)
    shared = shared.reshape(sections, kept + 3 * tokens, bottleneck)
    cross = shared[:, :kept].reshape(sections, sections, bottleneck, bottleneck)
    shared = shared[:, kept:].reshape(sections, 3, tokens, bottleneck)
    acts, slopes, branch = (shared[:, 0], shared[:, 1], shared[:, 2].astype(f32))

    grads = [None] * sections
    for s in range(sections - 1, -1, -1):
        grads[s] = (branch[s] * slopes[s].astype(f32)).astype(bf16)
        if s:
            step = mm("tm,smn->stn", grads[s], cross[:s, s])
            branch = branch[:s] + step
    grads = jnp.stack(grads)
    own_grad, own_act = (pick(grads, section), pick(acts, section))

    weight = jnp.where(order > section, 1.0, jnp.where(order == section, 0.5, 0.0)).astype(bf16)
    mixed = mm("stn,smn->tm", grads * weight[:, None, None], pick(cross, section, 1))
    mixed = (loss_down + mixed).astype(bf16).reshape(micro_count, tok_count, bottleneck)
    grad_micro = own_grad.reshape(micro_count, tok_count, bottleneck)
    step_gram = mm("btk,buk->btu", mixed, grad_micro)
    step_gram = step_gram + jnp.swapaxes(step_gram, 1, 2)
    acts_micro = acts.reshape(sections, micro_count, tok_count, bottleneck)
    act_grams = mm("sbtk,sbuk->sbtu", acts_micro, acts_micro)
    before = (order < section).astype(f32)
    products = (
        gram_in * mm("btk,buk->btu", grad_micro, grad_micro)
        + gram_loss * jnp.sum(act_grams, axis=0)
        + step_gram * jnp.sum(act_grams * before[:, None, None, None], axis=0)
    )
    example_rows = example_ids[:, 0]
    member = (example_rows[:, :, None] == jnp.arange(EX, dtype=jnp.int32)).astype(f32)
    across_u = jnp.sum(products[..., None] * member[:, None], axis=2)
    own_norms = jnp.sum(across_u * member, axis=1)
    summed = lax.psum(own_norms, "section")
    example_norms = jnp.sqrt(summed)[:, None, :]
    clip_scale = jnp.minimum(1.0, clip_bound * lax.rsqrt(summed))
    token_scale = jnp.sum(member * clip_scale[:, None, :], axis=-1).reshape(tokens, 1)

    scaled_grad = (own_grad.astype(f32) * token_scale).astype(bf16)
    scaled_act = (own_act.astype(f32) * token_scale).astype(bf16)
    rows = own_down.shape[0]
    firsts_down, firsts_up = first_pieces(rows)
    part_down, *firsts_down = gradient_part(flat_in, scaled_grad, firsts_down)
    part_up, *firsts_up = gradient_part(loss_full, scaled_act, firsts_up)
    firsts = firsts_down + firsts_up

    def after_clip(turn):
        if turn == 0:
            cross_up = mm("stm,tn->smn", grads, scaled_act)
            cross_up = jnp.where(later, cross_up, 0).astype(bf16)
            work["up"] = cross_up.reshape(sections * bottleneck, bottleneck)
        if turn == 3:
            work["up"] = spread(work["up"])
        if turn == 2:
            return []
        if turn == 5:
            work["up"] = collect(work["up"])
        return [work["up"]]

    downs, ups, (cross_up,) = scatter_all(part_down, part_up, firsts, rows, after_clip)
    cross_up = cross_up.reshape(sections, bottleneck, bottleneck)
    step_up = mm("skm,smn->kn", work["down_rows"], cross_up)
    new_down, new_up = fold(
        [(rows, downs + [(run_down[0], 0), (noise_down[0], 0)])],
        [(rows, ups + [(step_up, 0), (run_up[0], 0), (noise_up[0], 0)])],
        dtype=f32,
    )
    return (new_down[None], new_up[None], example_norms)


def solution(mesh):
    return jax.shard_map(
        shards,
        mesh=mesh,
        in_specs=(
            P("section", None, "dp", None, None),
            P(None, "dp", None),
            P(None, "dp", None, "section"),
            P("section", "dp", None),
            P("section", "dp", None),
            P("section", "dp", None),
            P("section", "dp", None),
            P("section", "dp", None),
            P("section", "dp", None),
        ),
        out_specs=(P("section", "dp", None), P("section", "dp", None), P(None, "dp", None)),
        check_vma=False,
    )
```

```python
import jax
import jax.numpy as jnp
from jax import lax
from jax.experimental import pallas as pl
from jax.experimental.pallas import tpu as pltpu
from jax.sharding import PartitionSpec as P

EX = 2
NZ, NY = 8, 4
NX, NC = 4, 2

clip_bound = 400.0
bf16 = jnp.bfloat16
f32 = jnp.float32


def shift_z(value, d):
    pairs = [(z * NY + y, (z + d) % NZ * NY + y) for z in range(NZ) for y in range(NY)]
    return lax.ppermute(value, "dp", pairs)


def shift_y(value, d):
    pairs = [(z * NY + y, z * NY + (y + d) % NY) for z in range(NZ) for y in range(NY)]
    return lax.ppermute(value, "dp", pairs)


def shift_x(value, d):
    pairs = [(x * NC + c, (x + d) % NX * NC + c) for x in range(NX) for c in range(NC)]
    return lax.ppermute(value, "section", pairs)


def swap_core(value):
    return lax.ppermute(value, "section", [(s, s ^ 1) for s in range(NX * NC)])


def pick(value, index, axis=0):
    return lax.dynamic_index_in_dim(value, index, axis, keepdims=False)


def put(buffer, value, index, axis=0):
    return lax.dynamic_update_index_in_dim(buffer, value, index, axis)


def put_at(buffer, piece, first, second):
    return lax.dynamic_update_slice(buffer, piece[None, None], (first, second, 0, 0))


def together(*moves, also=()):
    moved = tuple(move(value, *by) for move, value, *by in moves)
    return lax.optimization_barrier(moved + tuple(also))


class At:
    def __init__(self, value):
        self.value = value

    def __add__(self, other):
        return At(lambda p: self.value(p) + number(other, p))

    def __sub__(self, other):
        return At(lambda p: self.value(p) - number(other, p))

    def __rsub__(self, other):
        return At(lambda p: number(other, p) - self.value(p))

    def __mul__(self, other):
        return At(lambda p: self.value(p) * number(other, p))

    def __mod__(self, other):
        return At(lambda p: lax.rem(self.value(p), jnp.int32(other)))

    __radd__, __rmul__ = (__add__, __mul__)


def number(value, p):
    return value.value(p) if isinstance(value, At) else value


AT_X, AT_CORE, AT_Z, AT_Y = (At(lambda p, k=k: p[k]) for k in range(4))


def row(value, p):
    return pl.multiple_of(value.value(p), 16) if isinstance(value, At) else value


class Operands:
    def __init__(self):
        self.arrays = []

    def array(self, value):
        for k, known in enumerate(self.arrays):
            if known is value:
                return k
        self.arrays.append(value)
        return len(self.arrays) - 1

    def call(self, kernel, out_shape, out_specs, scratch, flops=0, moved=0, limit=57):
        section, place = (lax.axis_index("section"), lax.axis_index("dp"))
        here = jnp.stack([section // NC, section % NC, place // NY, place % NY]).astype(jnp.int32)
        def body(position, *refs):
            kernel([position[k] for k in range(4)], *refs)

        return pl.pallas_call(
            body,
            out_shape=out_shape,
            in_specs=[pl.BlockSpec(memory_space=pltpu.SMEM)]
            + [pl.BlockSpec(memory_space=pl.ANY)] * len(self.arrays),
            out_specs=out_specs,
            scratch_shapes=scratch,
            compiler_params=pltpu.CompilerParams(vmem_limit_bytes=limit << 20),
            cost_estimate=pl.CostEstimate(flops=flops, bytes_accessed=moved, transcendentals=0),
        )(here, *self.arrays)


def load(copies, sems, source, target):
    copies.append(pltpu.make_async_copy(source, target, sems.at[len(copies)]))
    copies[-1].start()


def pack(*jobs):
    held = Operands()
    plan = []
    for out, job in enumerate(jobs):
        low = 0
        for array, start, rows in job:
            plan.append((out, low, rows, held.array(array), start))
            low += rows
    shapes = [
        jax.ShapeDtypeStruct((sum(p[2] for p in job),) + job[0][0].shape[1:], job[0][0].dtype)
        for job in jobs
    ]
    count = len(held.arrays)

    def kernel(p, *refs):
        ins, outs = (refs[:count], refs[count : count + len(jobs)])
        buffers, (in_sems, out_sems) = (refs[count + len(jobs) : -2], refs[-2:])
        copies = []
        for out, low, rows, k, place in plan:
            source = ins[k].at[pl.ds(row(place, p), rows)]
            load(copies, in_sems, source, buffers[out].at[pl.ds(low, rows)])
        stores = []
        for out in range(len(jobs)):
            for copy, step in zip(copies, plan):
                if step[0] == out:
                    copy.wait()
            load(stores, out_sems, buffers[out], outs[out])
        for store in stores:
            store.wait()

    specs = [pl.BlockSpec(memory_space=pl.ANY)] * len(jobs)
    scratch = [pltpu.VMEM(t.shape, t.dtype) for t in shapes]
    scratch += [pltpu.SemaphoreType.DMA((len(plan),)), pltpu.SemaphoreType.DMA((len(jobs),))]
    moved = sum(2 * t.size * t.dtype.itemsize for t in shapes)
    return held.call(kernel, shapes, specs, scratch, 0, moved, 16)


def assemble(pieces, total):
    held = Operands()
    plan = [(held.array(a), low, rows, at) for a, low, rows, at in pieces]
    shape = jax.ShapeDtypeStruct((total,) + pieces[0][0].shape[1:], pieces[0][0].dtype)
    count = len(held.arrays)

    def kernel(p, *refs):
        ins = refs[:count]
        whole, buffer, sems, out_sem = refs[count:]
        copies = []
        for k, low, rows, at in plan:
            source = ins[k].at[pl.ds(row(low, p), rows)]
            load(copies, sems, source, buffer.at[pl.ds(row(at, p), rows)])
        for copy in copies:
            copy.wait()
        store = pltpu.make_async_copy(buffer, whole, out_sem)
        store.start()
        store.wait()

    spec = pl.BlockSpec(memory_space=pl.ANY)
    scratch = [
        pltpu.VMEM(shape.shape, shape.dtype),
        pltpu.SemaphoreType.DMA((len(plan),)),
        pltpu.SemaphoreType.DMA,
    ]
    return held.call(kernel, shape, spec, scratch, 0, 2 * shape.size * shape.dtype.itemsize, 16)


AROUND_X = (0, NX - 1, 1, 2)


def by_section(own, other, rows):
    pieces = []
    for k, d in enumerate(AROUND_X):
        place = (AT_X + d) % NX * NC
        pieces.append(own[k] + (rows, (place + AT_CORE) * rows))
        pieces.append(other[k] + (rows, (place + 1 - AT_CORE) * rows))
    return assemble(pieces, NX * NC * rows)


def section_gather(value, *also):
    before, after, across, mine, *also = together(
        (shift_x, value, 1), (shift_x, value, -1), (shift_x, value, 2), (swap_core, value), also=also
    )
    others = together((swap_core, before), (swap_core, after), (swap_core, across))
    own = [(v, 0) for v in (value, before, after, across)]
    return by_section(own, [(v, 0) for v in (mine,) + tuple(others)], value.shape[0]), *also


def fold(*jobs, dtype=bf16):
    held = Operands()
    plan, scratch, moved = ([], [], 0)
    for job in jobs:
        segments = []
        for rows, sources in job:
            names = []
            for array, start in sources:
                names.append((held.array(array), start, len(scratch)))
                scratch.append(pltpu.VMEM((rows, array.shape[1]), array.dtype))
                moved += rows * array.shape[1] * array.dtype.itemsize
            segments.append((rows, names))
        plan.append(segments)
    width = jobs[0][0][1][0][0].shape[1]
    shapes = [jax.ShapeDtypeStruct((sum(rows for rows, _ in job), width), dtype) for job in jobs]
    count, loads = (len(held.arrays), len(scratch))
    scratch = scratch + [pltpu.VMEM(t.shape, t.dtype) for t in shapes]
    scratch += [pltpu.SemaphoreType.DMA((loads,)), pltpu.SemaphoreType.DMA((len(jobs),))]

    def kernel(p, *refs):
        ins, outs = (refs[:count], refs[count : count + len(jobs)])
        buffers, results = (refs[count + len(jobs) :][:loads], refs[-2 - len(jobs) : -2])
        in_sems, out_sems = refs[-2:]
        copies = {}
        for segments in plan:
            for rows, names in segments:
                for k, place, n in names:
                    source = ins[k].at[pl.ds(row(place, p), rows)]
                    copies[n] = pltpu.make_async_copy(source, buffers[n], in_sems.at[n])
                    copies[n].start()
        stores = []
        for j, segments in enumerate(plan):
            low = 0
            for rows, names in segments:
                for _, _, n in names:
                    copies[n].wait()
                total = buffers[names[0][2]][...].astype(f32)
                for _, _, n in names[1:]:
                    total = total + buffers[n][...].astype(f32)
                results[j][low : low + rows, :] = total.astype(dtype)
                low += rows
            stores.append(pltpu.make_async_copy(results[j], outs[j], out_sems.at[j]))
            stores[-1].start()
        for store in stores:
            store.wait()

    specs = [pl.BlockSpec(memory_space=pl.ANY)] * len(jobs)
    return held.call(kernel, shapes, specs, scratch, 0, moved)


def gather_all(down, up, loss, beside):
    rows = down.shape[0]
    z, y = (AT_Z, AT_Y)
    none = (0, rows)

    q1, q3, q2, *grams = together(
        (shift_y, down, 1), (shift_y, down, -1), (shift_y, down, 2), also=beside(0)
    )
    quad_ys = (0, -1, 1, 2)
    (m,) = pack([(v,) + none for v in (down, q1, q3, q2, up)])
    f1, b1, w1, w3, w2 = together(
        (shift_z, m, 1),
        (shift_z, m, -1),
        (shift_x, down, 1),
        (shift_x, down, -1),
        (shift_x, down, 2),
    )
    (down_x,) = pack([(v,) + none for v in (down, w1, w3, w2)])
    f2, b2, loss_1, loss_3, down_other, *_ = together(
        (shift_z, f1, 1), (shift_z, b1, -1), (shift_x, loss, 1), (shift_x, loss, -1), (swap_core, down_x)
    )
    last = NY * rows
    (near,) = pack([(up, 0, rows)] + [(v, last, rows) for v in (f1, b1, f2, b2)])
    down_rows = by_section(
        [(v, 0) for v in (down, w1, w3, w2)], [(down_other, k * rows) for k in range(NX)], rows
    )
    f3, b3, near_1, near_3, loss_2, *_ = together(
        (shift_z, f2, 1),
        (shift_z, b2, -1),
        (shift_y, near, 1),
        (shift_y, near, -1),
        (shift_x, loss_1, 1),
        also=beside(3, down_rows),
    )
    cut = near.shape[0] // 32 * 16
    near_low, near_high, f3_low, b3_high = pack(
        [(near_1, 0, cut)],
        [(near_3, cut, near.shape[0] - cut)],
        [(f3, k * rows, rows) for k in range(3)],
        [(b3, k * rows, rows) for k in range(3, 5)],
    )
    f4, b4, near_low, near_high, swap_0, swap_1, swap_3, *_ = together(
        (shift_z, f3_low, 1),
        (shift_z, b3_high, -1),
        (shift_y, near_low, 1),
        (shift_y, near_high, -1),
        (swap_core, loss),
        (swap_core, loss_1),
        (swap_core, loss_3),
        also=beside(4),
    )

    def where(dz, dy):
        return ((z + (NZ + dz)) % NZ * NY + (y + (NY + dy)) % NY) * rows

    downs = []
    for array, dz in ((m, 0), (f1, -1), (b1, 1), (f2, -2), (b2, 2), (f3, -3), (b3, 3)):
        downs += [(array, k * rows, rows, where(dz, dy)) for k, dy in enumerate(quad_ys)]
    downs += [(f4, k * rows, rows, where(4, quad_ys[k])) for k in range(3)]
    downs += [(b4, 0, rows, where(4, quad_ys[3]))]

    (far,) = pack([(f3, last, rows), (b3, last, rows), (b4, rows, rows)])
    far_1, far_3, swap_2, *_ = together(
        (shift_y, far, 1), (shift_y, far, -1), (swap_core, loss_2), also=beside(5, downs)
    )
    near_zs, far_zs = ((0, -1, 1, -2, 2), (-3, 3, 4))

    def quarter(dy):
        return (y + (NY + dy)) % NY * rows

    ups_near, ups_far = ([], [])
    for array, dy in ((near, 0), (near_1, -1), (near_3, 1)):
        ups_near += [(array, k * rows, rows, k * last + quarter(dy)) for k in range(5)]
    split = cut - 2 * rows
    ups_near += [(near_low, k * rows, rows, k * last + quarter(2)) for k in range(2)]
    ups_near += [(near_low, 2 * rows, split, 2 * last + quarter(2))]
    ups_near += [(near_high, 0, rows - split, 2 * last + quarter(2) + split)]
    ups_near += [
        (near_high, (k - 2) * rows - split, rows, k * last + quarter(2)) for k in range(3, 5)
    ]
    near_at = [(z + (NZ + dz)) % NZ for dz in near_zs]
    far_at = [(z + (NZ + dz)) % NZ for dz in far_zs]
    losses = []
    pieces = ((loss, swap_0), (loss_1, swap_1), (loss_3, swap_3), (loss_2, swap_2))
    for (piece, swapped), d in zip(pieces, AROUND_X):
        place = (AT_X + d) % NX * NC
        losses += [(piece, place + AT_CORE), (swapped, place + 1 - AT_CORE)]

    far_2, *done = together((shift_y, far_1, 1), also=beside(6, losses, ups_near, near_at))
    for array, dy in ((far, 0), (far_1, -1), (far_3, 1), (far_2, 2)):
        ups_far += [(array, k * rows, rows, k * last + quarter(dy)) for k in range(3)]
    return downs, (ups_far, far_at), done + grams


def gelu_parts(hidden):
    normal_cdf = 0.5 * (1.0 + lax.erf(hidden * 0.7071067811865476))
    normal_pdf = jnp.exp(-0.5 * hidden * hidden) * 0.3989422804014327
    return (hidden * normal_cdf, normal_cdf + hidden * normal_pdf)


def project_inputs(inputs, downs):
    held = Operands()
    tokens, depth = inputs.shape
    width = downs[0][0].shape[1]
    n_in = held.array(inputs)
    plan = [(held.array(a), low, rows, at) for a, low, rows, at in downs]
    count = len(held.arrays)
    parts = 4
    chunk = depth // parts

    def kernel(p, *refs):
        ins = refs[:count]
        act, slope, xs, wd, sems = refs[count:]
        copies = []
        for k, low, rows, at in plan:
            load(copies, sems, ins[k].at[pl.ds(row(low, p), rows)], wd.at[pl.ds(row(at, p), rows)])
        for j in range(parts):
            load(copies, sems, ins[n_in].at[:, pl.ds(j * chunk, chunk)], xs.at[j])
        for copy in copies[: len(plan)]:
            copy.wait()
        value = jnp.zeros((tokens, width), f32)
        for j in range(parts):
            copies[len(plan) + j].wait()
            weights = wd[j * chunk : (j + 1) * chunk, :]
            value = value + jnp.dot(xs[j], weights, preferred_element_type=f32)
        gated, rise = gelu_parts(value)
        act[...] = gated.astype(bf16)
        slope[...] = rise.astype(bf16)

    shapes = [jax.ShapeDtypeStruct((tokens, width), bf16)] * 2
    scratch = [
        pltpu.VMEM((parts, tokens, chunk), bf16),
        pltpu.VMEM((depth, width), bf16),
        pltpu.SemaphoreType.DMA((len(plan) + parts,)),
    ]
    specs = [pl.BlockSpec(memory_space=pltpu.VMEM)] * 2
    return held.call(kernel, shapes, specs, scratch, 2 * tokens * depth * width, 9 << 20)


def project_near(losses, ups, at):
    held = Operands()
    tokens, slice_width = losses[0][0].shape
    width = ups[0][0].shape[1]
    loss_at = [(held.array(a), place) for a, place in losses]
    plan = [(held.array(a), low, rows, to) for a, low, rows, to in ups]
    count = len(held.arrays)
    n_loss = len(losses)

    def kernel(p, *refs):
        ins = refs[:count]
        out, whole, g, wu, sems, out_sem = refs[count:]
        copies = []
        for k, place in loss_at:
            load(copies, sems, ins[k], g.at[number(place, p)])
        for k, low, rows, to in plan:
            load(copies, sems, ins[k].at[pl.ds(row(low, p), rows)], wu.at[pl.ds(row(to, p), rows)])
        for copy in copies[:n_loss]:
            copy.wait()
        store = pltpu.make_async_copy(g, whole, out_sem)
        store.start()
        for copy in copies[n_loss:]:
            copy.wait()
        value = jnp.zeros((tokens, width), f32)
        for j in range(len(at)):
            weights = wu[j * slice_width : (j + 1) * slice_width, :]
            value = value + jnp.dot(g[number(at[j], p)], weights, preferred_element_type=f32)
        out[...] = value
        store.wait()

    shapes = [
        jax.ShapeDtypeStruct((tokens, width), f32),
        jax.ShapeDtypeStruct((n_loss, tokens, slice_width), bf16),
    ]
    scratch = [
        pltpu.VMEM(shapes[1].shape, bf16),
        pltpu.VMEM((len(at) * slice_width, width), bf16),
        pltpu.SemaphoreType.DMA((n_loss + len(plan),)),
        pltpu.SemaphoreType.DMA,
    ]
    specs = [pl.BlockSpec(memory_space=pltpu.VMEM), pl.BlockSpec(memory_space=pl.ANY)]
    return held.call(
        kernel, shapes, specs, scratch, 2 * tokens * len(at) * slice_width * width, 12 << 20
    )


def project_slices(start, loss_full, weights, at, dtype):
    held = Operands()
    _, tokens, slice_width = loss_full.shape
    width = weights[0][0].shape[1]
    n_loss, n_start = (held.array(loss_full), held.array(start))
    plan = [(held.array(a), low, rows, to) for a, low, rows, to in weights]
    count = len(held.arrays)
    slices = len(at)

    def kernel(p, *refs):
        ins = refs[:count]
        out, g, w, total, sems = refs[count:]
        copies = []
        load(copies, sems, ins[n_start], total)
        for j in range(slices):
            load(copies, sems, ins[n_loss].at[number(at[j], p)], g.at[j])
        for k, low, rows, to in plan:
            load(copies, sems, ins[k].at[pl.ds(row(low, p), rows)], w.at[pl.ds(row(to, p), rows)])
        for copy in copies:
            copy.wait()
        value = total[...]
        for j in range(slices):
            part = w[j * slice_width : (j + 1) * slice_width, :]
            value = value + jnp.dot(g[j], part, preferred_element_type=f32)
        out[...] = value.astype(dtype)

    shape = jax.ShapeDtypeStruct((tokens, width), dtype)
    scratch = [
        pltpu.VMEM((slices, tokens, slice_width), bf16),
        pltpu.VMEM((slices * slice_width, width), bf16),
        pltpu.VMEM((tokens, width), f32),
        pltpu.SemaphoreType.DMA((1 + slices + len(plan),)),
    ]
    spec = pl.BlockSpec(memory_space=pltpu.VMEM)
    moved = slices * slice_width * (tokens + width) * 2
    return held.call(kernel, shape, spec, scratch, 2 * tokens * slices * slice_width * width, moved)


def gradient_part(values, scaled, firsts):
    held = Operands()
    tokens, width = scaled.shape
    depth = values.size // tokens
    sliced = values.ndim == 3
    parts = values.shape[0] if sliced else 4
    wide = depth // parts
    n_values, n_scaled = (held.array(values), held.array(scaled))
    plan = []
    for out, job in enumerate(firsts):
        low = 0
        for start, rows in job:
            plan.append((out, low, rows, start))
            low += rows
    count = len(held.arrays)

    def kernel(p, *refs):
        ins, outs = (refs[:count], refs[count : count + 1 + len(firsts)])
        xs, sh, whole, in_sems, out_sems = refs[count + 1 + len(firsts) :]
        copies = []
        load(copies, in_sems, ins[n_scaled], sh)
        for j in range(parts):
            source = ins[n_values].at[j] if sliced else ins[n_values].at[:, pl.ds(j * wide, wide)]
            load(copies, in_sems, source, xs.at[j])
        stores = []
        over_tokens = (((0,), (0,)), ((), ()))
        copies[0].wait()
        factor = sh[...]
        for j in range(parts):
            copies[1 + j].wait()
            part = lax.dot_general(xs[j], factor, over_tokens, preferred_element_type=f32)
            span = pl.ds(j * wide, wide)
            whole[span, :] = part.astype(bf16)
            load(stores, out_sems, whole.at[span], outs[0].at[span])
        for out, low, rows, place in plan:
            source = whole.at[pl.ds(row(place, p), rows)]
            load(stores, out_sems, source, outs[1 + out].at[pl.ds(low, rows)])
        for store in stores:
            store.wait()

    shapes = [jax.ShapeDtypeStruct((depth, width), bf16)]
    shapes += [jax.ShapeDtypeStruct((sum(q[1] for q in job), width), bf16) for job in firsts]
    scratch = [
        pltpu.VMEM((parts, tokens, wide), bf16),
        pltpu.VMEM((tokens, width), bf16),
        pltpu.VMEM((depth, width), bf16),
        pltpu.SemaphoreType.DMA((1 + parts,)),
        pltpu.SemaphoreType.DMA((parts + len(plan),)),
    ]
    specs = [pl.BlockSpec(memory_space=pl.ANY)] * len(shapes)
    return held.call(kernel, shapes, specs, scratch, 2 * tokens * depth * width, 9 << 20)


FAR, NEAR = ((3, -3, 4), (0, 1, -1, 2, -2))


def first_pieces(rows):
    z, y = (AT_Z, AT_Y)
    half = NY * rows // 2
    cut = len(FAR) * rows // 32 * 16
    opposite = (z + NZ // 2) % NZ * NY * rows
    blocks = [((z + (NZ + k)) % NZ * NY + (y + 2) % NY) * rows for k in FAR]
    split = cut - rows
    return (
        (((opposite, half),), ((opposite + half, half),)),
        (
            ((blocks[0], rows), (blocks[1], split)),
            ((blocks[1] + split, rows - split), (blocks[2], rows)),
        ),
    )


def scatter_all(pd, pu, firsts, rows, beside):
    z, y = (AT_Z, AT_Y)
    cut = rows // 32 * 16
    full = NY * rows
    half = full // 2
    far_cut = len(FAR) * rows // 32 * 16
    split = far_cut - rows

    def dz(k):
        return (z + (NZ + k)) % NZ * full

    def uz(k, d):
        return ((z + (NZ + k)) % NZ * NY + (y + (NY + d)) % NY) * rows

    f0, b0, u0, d0 = firsts
    rest = rows - split
    f, b, *_ = together((shift_z, f0, 1), (shift_z, b0, -1))
    u, d, *_ = together((shift_y, u0, 1), (shift_y, d0, -1))
    f, b = fold(
        [(half, [(pd, dz(3)), (f, 0)]), (half, [(pd, dz(3) + half)])],
        [(half, [(pd, dz(-3))]), (half, [(pd, dz(-3) + half), (b, 0)])],
    )
    f, b, *_ = together((shift_z, f, 1), (shift_z, b, -1))
    u, d, across = fold(
        [
            (rows, [(pu, uz(FAR[0], 1)), (u, 0)]),
            (split, [(pu, uz(FAR[1], 1)), (u, rows)]),
            (rest, [(pu, uz(FAR[1], 1) + split)]),
            (rows, [(pu, uz(FAR[2], 1))]),
        ],
        [
            (rows, [(pu, uz(FAR[0], -1))]),
            (split, [(pu, uz(FAR[1], -1))]),
            (rest, [(pu, uz(FAR[1], -1) + split), (d, 0)]),
            (rows, [(pu, uz(FAR[2], -1)), (d, rest)]),
        ],
        [(rows, [(pu, uz(k, 2))]) for k in NEAR],
    )
    uf, df, *_ = together((shift_y, u, 1), (shift_y, d, -1), also=beside(0))

    def far(k, low):
        return [(pu, uz(FAR[k], 0) + low), (uf, k * rows + low), (df, k * rows + low)]

    f, b = fold(
        [(full, [(pd, dz(2)), (f, 0)]), (cut, far(2, 0))],
        [(full, [(pd, dz(-2)), (b, 0)]), (rows - cut, far(2, cut))],
    )
    (u,) = together((shift_y, across, 1))
    f, b, *_ = together((shift_z, f, 1), (shift_z, b, -1), also=beside(2))
    u, d = fold(
        [(rows, [(pu, uz(k, 1)), (u, n * rows)]) for n, k in enumerate(NEAR)],
        [(rows, [(pu, uz(k, -1))]) for k in NEAR],
    )
    un, dn, *_ = together((shift_y, u, 1), (shift_y, d, -1), also=beside(3))
    f, b = fold(
        [(full, [(pd, dz(1)), (f, 0)]), (cut, far(0, 0) + [(f, full)]), (rows - cut, far(0, cut))],
        [(full, [(pd, dz(-1)), (b, 0)]), (cut, far(1, 0)), (rows - cut, far(1, cut) + [(b, full)])],
    )
    f, b, *_ = together((shift_z, f, 1), (shift_z, b, -1))

    def near(n):
        return [(pu, uz(NEAR[n], 0)), (un, n * rows), (dn, n * rows)]

    def own(d):
        low = (y + (NY + d)) % NY * rows
        return [(pd, dz(0) + low), (f, low), (b, low)]

    fz, bz, e1, e2, e3 = fold(
        [(rows, near(3) + [(f, full)])],
        [(rows, near(4) + [(b, full)])],
        [(rows, own(1))],
        [(rows, own(-1))],
        [(rows, own(2))],
    )
    fz, bz = together((shift_z, fz, 1), (shift_z, bz, -1))
    e1, e2, e3 = together((shift_y, e1, 1), (shift_y, e2, -1), (shift_y, e3, 2))
    fz, bz = fold([(rows, near(1) + [(fz, 0)])], [(rows, near(2) + [(bz, 0)])])
    fz, bz, *done = together((shift_z, fz, 1), (shift_z, bz, -1), also=beside(5))
    return own(0) + [(e1, 0), (e2, 0), (e3, 0)], near(0) + [(fz, 0), (bz, 0)], done


def spread(parts):
    count = lax.axis_size("dp")
    rows, width = parts.shape
    split = parts.astype(bf16).reshape(count, rows // count, width)
    return lax.all_to_all(split, "dp", 0, 0)


def collect(arrived):
    summed = jnp.sum(arrived.astype(f32), axis=0).astype(bf16)
    sent = jnp.broadcast_to(summed[None], arrived.shape)
    return lax.all_to_all(sent, "dp", 0, 0).reshape(-1, arrived.shape[2])


def mm(subs, *operands):
    return jnp.einsum(subs, *operands, preferred_element_type=f32)


def shards(
    saved_inputs, example_ids, loss_grads, w_down, w_up, run_down, run_up, noise_down, noise_up
):
    sections = lax.axis_size("section")
    section = lax.axis_index("section")
    order = jnp.arange(sections)
    inputs = saved_inputs[0, :, 0]
    micro_count, tok_count, model_width = inputs.shape
    tokens = micro_count * tok_count
    bottleneck = w_down.shape[2]
    flat_in = inputs.reshape(tokens, model_width)
    loss_own = loss_grads[:, 0]
    slice_width = loss_own.shape[2]
    own_down, own_up = (w_down[0], w_up[0])

    later = (order > section)[:, None, None]
    work = {}

    def before_chain(turn, *given):
        if turn == 0:
            return [mm("btd,bud->btu", v, v) for v in (inputs, loss_own)]
        if turn == 3:
            down_rows = given[0].reshape((sections,) + own_down.shape)
            cross = jnp.where(
                later, mm("skm,kn->smn", down_rows, own_up), mm("skm,kn->smn", down_rows, own_down)
            )
            work["down_rows"] = down_rows
            work["cross"] = cross.astype(bf16).reshape(sections * bottleneck, bottleneck)
            return [work["cross"]]
        if turn == 4:
            work["cross"] = spread(work["cross"])
            return [work["cross"]]
        if turn == 5:
            work["act"], work["slope"] = project_inputs(flat_in, *given)
            return [work["act"], work["slope"]]
        work["cross"] = collect(work["cross"])
        near = project_near(*given)
        return [work["act"], work["slope"], work["cross"], *near]

    downs, (ups_far, far_at), done = gather_all(
        own_down, own_up, loss_own.reshape(tokens, slice_width), before_chain
    )
    own_act, own_slope, cross, loss_up, loss_full, gram_in, gram_loss = done
    loss_up = project_slices(loss_up, loss_full, ups_far, far_at, bf16)
    kept = cross.shape[0]
    (shared,) = pack([(cross, 0, kept)] + [(v, 0, tokens) for v in (own_act, own_slope, loss_up)])
    none = jnp.zeros((tokens, bottleneck), f32)
    loss_down = project_slices(none, loss_full, downs, list(range(sections)), f32)
    shared, loss_down = section_gather(shared, loss_down)
    shared = shared.reshape(sections, kept + 3 * tokens, bottleneck)
    cross = shared[:, :kept].reshape(sections, sections, bottleneck, bottleneck)
    shared = shared[:, kept:].reshape(sections, 3, tokens, bottleneck)
    acts, slopes, branch = (shared[:, 0], shared[:, 1], shared[:, 2].astype(f32))

    grads = [None] * sections
    for s in range(sections - 1, -1, -1):
        grads[s] = (branch[s] * slopes[s].astype(f32)).astype(bf16)
        if s:
            step = mm("tm,smn->stn", grads[s], cross[:s, s])
            branch = branch[:s] + step
    grads = jnp.stack(grads)
    own_grad, own_act = (pick(grads, section), pick(acts, section))

    weight = jnp.where(order > section, 1.0, jnp.where(order == section, 0.5, 0.0)).astype(bf16)
    mixed = mm("stn,smn->tm", grads * weight[:, None, None], pick(cross, section, 1))
    mixed = (loss_down + mixed).astype(bf16).reshape(micro_count, tok_count, bottleneck)
    grad_micro = own_grad.reshape(micro_count, tok_count, bottleneck)
    step_gram = mm("btk,buk->btu", mixed, grad_micro)
    step_gram = step_gram + jnp.swapaxes(step_gram, 1, 2)
    acts_micro = acts.reshape(sections, micro_count, tok_count, bottleneck)
    act_grams = mm("sbtk,sbuk->sbtu", acts_micro, acts_micro)
    before = (order < section).astype(f32)
    products = (
        gram_in * mm("btk,buk->btu", grad_micro, grad_micro)
        + gram_loss * jnp.sum(act_grams, axis=0)
        + step_gram * jnp.sum(act_grams * before[:, None, None, None], axis=0)
    )
    example_rows = example_ids[:, 0]
    member = (example_rows[:, :, None] == jnp.arange(EX, dtype=jnp.int32)).astype(f32)
    across_u = jnp.sum(products[..., None] * member[:, None], axis=2)
    own_norms = jnp.sum(across_u * member, axis=1)
    sent = jnp.broadcast_to(own_norms.reshape(1, -1, 1), (sections, own_norms.size, 128))
    summed = jnp.sum(lax.all_to_all(sent, "section", 0, 0), axis=0)[:, 0].reshape(own_norms.shape)
    example_norms = jnp.sqrt(summed)[:, None, :]
    clip_scale = jnp.minimum(1.0, clip_bound * lax.rsqrt(summed))
    token_scale = jnp.sum(member * clip_scale[:, None, :], axis=-1).reshape(tokens, 1)

    scaled_grad = (own_grad.astype(f32) * token_scale).astype(bf16)
    scaled_act = (own_act.astype(f32) * token_scale).astype(bf16)
    rows = own_down.shape[0]
    firsts_down, firsts_up = first_pieces(rows)
    part_down, *firsts_down = gradient_part(flat_in, scaled_grad, firsts_down)
    part_up, *firsts_up = gradient_part(loss_full, scaled_act, firsts_up)
    firsts = firsts_down + firsts_up

    def after_clip(turn):
        if turn == 0:
            cross_up = mm("stm,tn->smn", grads, scaled_act)
            cross_up = jnp.where(later, cross_up, 0).astype(bf16)
            work["up"] = cross_up.reshape(sections * bottleneck, bottleneck)
        if turn == 3:
            work["up"] = spread(work["up"])
        if turn == 2:
            return []
        if turn == 5:
            cross_up = collect(work["up"]).reshape(sections, bottleneck, bottleneck)
            work["up"] = mm("skm,smn->kn", work["down_rows"], cross_up)
        return [work["up"]]

    downs, ups, (step_up,) = scatter_all(part_down, part_up, firsts, rows, after_clip)
    new_down, new_up = fold(
        [(rows, downs + [(run_down[0], 0), (noise_down[0], 0)])],
        [(rows, ups + [(step_up, 0), (run_up[0], 0), (noise_up[0], 0)])],
        dtype=f32,
    )
    return (new_down[None], new_up[None], example_norms)


def solution(mesh):
    return jax.shard_map(
        shards,
        mesh=mesh,
        in_specs=(
            P("section", None, "dp", None, None),
            P(None, "dp", None),
            P(None, "dp", None, "section"),
            P("section", "dp", None),
            P("section", "dp", None),
            P("section", "dp", None),
            P("section", "dp", None),
            P("section", "dp", None),
            P("section", "dp", None),
        ),
        out_specs=(P("section", "dp", None), P("section", "dp", None), P(None, "dp", None)),
        check_vma=False,
    )
```
